32 devices in a mesh: section: 16 (over z, y, x), tp: 2 (over core).
Axes of the slice: x: 2, y: 2, z: 4, core: 2. Of those that a mesh axis runs over, the one named last changes fastest.
Arguments:
- preview: bfloat16 [256, 8192], P('section', 'tp'), may hold values from -6 to 6
- row_owner: int32 [256], P('section'), may hold values from 0 to 31, never falling along the last dimension, each value on 1 to 32 neighbouring positions
- norm_gain: float32 [8192], P('tp'), may hold values from 0.25 to 1.75
- w_gate: bfloat16 [28672, 8192], P('section', 'tp'), may hold values from -0.0625 to 0.0625
- w_up: bfloat16 [28672, 8192], P('section', 'tp'), may hold values from -0.0625 to 0.0625
- w_down: bfloat16 [28672, 8192], P('section', 'tp'), may hold values from -0.03125 to 0.03125
- score_vec: float32 [8192], P('tp'), may hold values from -0.75 to 0.75
Outputs:
- verified: bfloat16 [256, 8192], P('section', 'tp')
- scores: float32 [32], replicated
The draws below stay inside these ranges and needn't reach their ends.
Inputs may be any that keep to these rules, and one draw needn't show every extreme that they name: row_owner never falls along the rows; every candidate owns 1 to 32 consecutive rows, some candidate exactly 32.
All inputs are finite; a program needn't handle non-finite values.
Results may differ from the reference program's by a relative error of at most 0.017.
Values may be sent and summed in bfloat16 or wider, within the bound.
No kernel may reach another device: no remote copies, remote signals or barrier semaphores. Data moves between devices by JAX's collectives and lax.ppermute only.
A program may use at most 128 MiB of HBM per device.

```python
import math
import jax
import jax.numpy as jnp
import numpy as np
from jax import lax

D = 8192
FF = 28672
CAND = 32
ROWS = 256
N_TP = 2


def shard_levels(key, extent, shards, low, high):
    def one(position, parts):
        steps = jax.random.uniform(jax.random.fold_in(jax.random.fold_in(key, 6), position), (parts,), jnp.float32, low / len(shards), high / len(shards))
        return jnp.repeat(jnp.exp(steps), extent[position] // parts).reshape((-1,) + (1,) * (len(extent) - position - 1))

    gain = one(*shards[0])
    for cut in shards[1:]:
        gain = gain * one(*cut)
    return gain


def split_up(number_of, total, most, slope):
    loads = [(1 << 20) // math.isqrt(rank ** slope) + 1 for rank in range(2, number_of + 1)]
    rest, given = total - most - (number_of - 1), [1] * (number_of - 1)
    while rest > 0:
        free = [i for i in range(number_of - 1) if given[i] < most]
        pool, budget = sum([loads[i] for i in free]), rest
        for i in free:
            more = min(most - given[i], max(1, budget * loads[i] // pool), rest)
            given[i] = given[i] + more
            rest = rest - more
    return np.array([most] + given)


def ragged(stream_key, amount, total, reach, slope):
    if amount == 2:
        one = jax.random.randint(stream_key, (), max(1, total - reach), min(reach, total - 1) + 1)
        return jnp.stack([one, total - one])
    sizes = jnp.asarray(split_up(amount, total, reach, slope), jnp.int32)
    twos = (amount - 1) // 2
    donor, taker = sizes[1:1 + 2 * twos:2], sizes[2:2 + 2 * twos:2]
    room = jnp.minimum(donor - 1, reach - taker)
    shifted = jax.random.randint(jax.random.fold_in(stream_key, 1), (twos,), 0, 1 << 20) % (room + 1)
    sizes = sizes.at[1:1 + 2 * twos:2].set(donor - shifted).at[2:2 + 2 * twos:2].set(taker + shifted)
    return sizes[jax.random.permutation(jax.random.fold_in(stream_key, 2), amount)]


def gaussian(stream_key, shape, scale, limit, pieces=(), held_as=jnp.bfloat16):
    level = shard_levels(stream_key, shape, pieces, -0.22, 0.18) if pieces else 1.0
    result = jax.random.normal(stream_key, shape, jnp.float32) * scale * level
    return jnp.minimum(jnp.maximum(result, -limit), limit).astype(held_as)


def setup_inputs(seed: int = 0) -> dict:
    splits = jax.random.split(jax.random.key(seed), 8)
    preview = gaussian(splits[0], (ROWS, D), 1.0, 6.0, ((0, 16), (1, 2)))
    row_owner = jnp.searchsorted(jnp.cumsum(ragged(splits[1], CAND, ROWS, ROWS // 8, 2)), jnp.arange(ROWS), side="right").astype(jnp.int32)
    norm_gain = jnp.clip(1.0 + 0.15 * jax.random.normal(splits[2], (D,), jnp.float32), 0.25, 1.75)
    w_gate = gaussian(splits[3], (FF, D), D ** -0.5, 0.0625, ((0, 16), (1, 2)))
    w_up = gaussian(splits[4], (FF, D), D ** -0.5, 0.0625, ((0, 16), (1, 2)))
    w_down = gaussian(splits[5], (FF, D), FF ** -0.5, 0.03125, ((0, 16), (1, 2)))
    score_vec = gaussian(splits[6], (D,), 64 ** -0.5, 0.75, ((0, 2),), jnp.float32)
    return {"preview": preview, "row_owner": row_owner, "norm_gain": norm_gain, "w_gate": w_gate, "w_up": w_up, "w_down": w_down, "score_vec": score_vec}


def reference(preview, row_owner, norm_gain, w_gate, w_up, w_down, score_vec):
    resid = preview.astype(jnp.float32)
    mean_sq = lax.optimization_barrier(jnp.mean(resid * resid, axis=1, keepdims=True))
    normed = (resid * lax.rsqrt(mean_sq + 1e-05) * norm_gain[None, :]).astype(jnp.bfloat16)
    width = D // N_TP
    dims = (((1,), (1,)), ((), ()))
    gate = jnp.zeros((ROWS, FF), jnp.float32)
    up = jnp.zeros((ROWS, FF), jnp.float32)
    for block in range(N_TP):
        lo = block * width
        part_x = normed[:, lo:lo + width]
        gate = gate + lax.dot_general(part_x, w_gate[:, lo:lo + width], dims, preferred_element_type=jnp.float32).astype(jnp.bfloat16).astype(jnp.float32)
        up = up + lax.dot_general(part_x, w_up[:, lo:lo + width], dims, preferred_element_type=jnp.float32).astype(jnp.bfloat16).astype(jnp.float32)
    hidden = (jax.nn.silu(gate) * up).astype(jnp.bfloat16)
    verified = (resid + jnp.dot(hidden, w_down, preferred_element_type=jnp.float32)).astype(jnp.bfloat16)
    row_score = jnp.dot(verified.astype(jnp.float32), score_vec, precision=lax.Precision.HIGHEST)
    member = (row_owner[None, :] == jnp.arange(CAND, dtype=jnp.int32)[:, None]).astype(jnp.float32)
    totals = jnp.dot(member, row_score, precision=lax.Precision.HIGHEST)
    counts = lax.optimization_barrier(jnp.sum(member, axis=1))
    return (verified, totals / counts)
```

```python
import jax
import jax.numpy as jnp
from jax import lax
from jax.sharding import PartitionSpec as P

CAND = 32
LANES = 128
BOTH = ("section", "tp")
F32 = jnp.float32
BF16 = jnp.bfloat16


def cat(*parts):
    return jnp.concatenate(parts, axis=0)


def add(a, b):
    return (a.astype(F32) + b.astype(F32)).astype(BF16)


def build(n, tp):
    def swap(v, even, odd=None):
        odd = even if odd is None else odd
        pairs = [(s * tp + t, (s ^ (odd if t % 2 else even)) * tp + t) for s in range(n) for t in range(tp)]
        return lax.ppermute(v, BOTH, pairs)

    long_bits = [8 << i for i in range((n // 8).bit_length() - 1)]

    def gather_quad(g):
        a = swap(g, 1, 2)
        g = cat(g, a)
        return cat(g, swap(g, 2, 1))

    def gather(own):
        rows = own.shape[0]
        far = own
        for bit in long_bits:
            far = cat(far, swap(far, bit))
        far = far[rows:]
        near = cat(own, swap(own, 4))
        far = cat(far, swap(far, 4))
        return cat(gather_quad(near), gather_quad(far))

    def swap_middle(v):
        rows = v.shape[0] // n
        out, at = [], 0
        for length in (8 * rows, v.shape[0] - 8 * rows):
            q = length // 4
            out += [v[at + i * q : at + (i + 1) * q] for i in (0, 2, 1, 3)]
            at += length
        return cat(*out)

    def scatter_quad(v):
        h = v.shape[0] // 2
        v = add(v[:h], swap(v[h:], 2, 1))
        h //= 2
        return add(v[:h], swap(v[h:], 1, 2))

    def scatter(v):
        rows = v.shape[0] // n
        far = scatter_quad(v[8 * rows :])
        near = scatter_quad(v[: 8 * rows])
        h = far.shape[0] // 2
        far = add(far[:h], swap(far[h:], 4))
        near = add(near[:rows], swap(near[rows:], 4))
        v = cat(near, far)
        for bit in reversed(long_bits):
            h = v.shape[0] // 2
            got = swap(v[h:], bit)
            v = add(v[:h], got) if h > rows else v[:h].astype(F32) + got.astype(F32)
        return v

    def sum_sections(v):
        for bit in [1 << i for i in range(n.bit_length() - 1)]:
            v = v + swap(v, bit)
        return v

    def tp_swap(v):
        return lax.ppermute(v, "tp", [(t, t ^ 1) for t in range(tp)])

    def tp_sum(v):
        if tp == 2:
            return v.astype(F32) + swap_middle(tp_swap(v)).astype(F32)
        t = lax.axis_index("tp") % 2
        both = lax.psum(jnp.stack([jnp.where(t == 0, v, 0), jnp.where(t == 1, v, 0)]), "tp").astype(F32)
        mine = jnp.where(t == 0, both[0], both[1])
        return mine + swap_middle(jnp.where(t == 0, both[1], both[0]))

    def shards(preview, row_owner, norm_gain, w_gate, w_up, w_down, score_vec):
        width = preview.shape[1]
        dims = (((1,), (1,)), ((), ()))
        owner_lanes = jnp.broadcast_to(row_owner.astype(BF16)[:, None], (row_owner.shape[0], LANES))
        both = gather(jnp.concatenate([preview, owner_lanes], axis=1))
        rows_all = both[:, :width].astype(F32)
        owner = both[:, width].astype(jnp.int32)
        member = (owner[:, None] == jnp.arange(CAND, dtype=jnp.int32)[None, :]).astype(F32)
        x = (rows_all * norm_gain[None, :]).astype(BF16)
        sq = tp_sum(jnp.sum(rows_all * rows_all, axis=1)[:, None])
        scale = lax.rsqrt(sq / (width * tp) + 1e-05)
        units = w_gate.shape[0]
        gate = lax.dot_general(x, w_gate, dims, preferred_element_type=F32).astype(BF16)
        up = lax.dot_general(x, w_up, dims, preferred_element_type=F32).astype(BF16)
        gate_up = tp_sum(jnp.concatenate([gate, up], axis=1)) * scale
        hidden = (jax.nn.silu(gate_up[:, :units]) * gate_up[:, units:]).astype(BF16)
        unit_score = jnp.sum(w_down.astype(F32) * score_vec[None, :], axis=1)
        rows = preview.shape[0]
        row_part = jnp.sum(hidden.astype(F32) * unit_score[None, :], axis=1)
        own_part = jnp.sum(preview.astype(F32) * score_vec[None, :], axis=1)
        totals = jnp.sum(member * row_part[:, None], axis=0) + jnp.sum(member[:rows] * own_part[:, None], axis=0)
        totals = tp_swap(totals) + totals if tp == 2 else lax.psum(totals, "tp")
        totals = sum_sections(totals)
        scores = totals / jnp.sum(member, axis=0)
        down = jnp.dot(hidden, w_down, preferred_element_type=F32).astype(BF16)
        verified = (preview.astype(F32) + scatter(down)).astype(BF16)
        return verified, scores

    return shards


def solution(mesh):
    placed = (
        P("section", "tp"),
        P("section"),
        P("tp"),
        P("section", "tp"),
        P("section", "tp"),
        P("section", "tp"),
        P("tp"),
    )
    return jax.shard_map(
        build(mesh.shape["section"], mesh.shape["tp"]),
        mesh=mesh,
        in_specs=placed,
        out_specs=(P("section", "tp"), P()),
        check_vma=False,
    )
```

```python
import jax
import jax.numpy as jnp
from jax import lax
from jax.experimental import pallas as pl
from jax.experimental.pallas import tpu as pltpu
from jax.sharding import PartitionSpec as P

CAND = 32
LANES = 128
BOTH = ("section", "tp")
F32 = jnp.float32
BF16 = jnp.bfloat16


def cat(*parts):
    return jnp.concatenate(parts, axis=0)


def add(a, b):
    return (a.astype(F32) + b.astype(F32)).astype(BF16)


def general(n, tp):
    def swap(v, even, odd=None):
        odd = even if odd is None else odd
        pairs = [(s * tp + t, (s ^ (odd if t % 2 else even)) * tp + t) for s in range(n) for t in range(tp)]
        return lax.ppermute(v, BOTH, pairs)

    long_bits = [8 << i for i in range((n // 8).bit_length() - 1)]

    def gather_quad(g):
        a = swap(g, 1, 2)
        g = cat(g, a)
        return cat(g, swap(g, 2, 1))

    def gather(own):
        rows = own.shape[0]
        far = own
        for bit in long_bits:
            far = cat(far, swap(far, bit))
        far = far[rows:]
        near = cat(own, swap(own, 4))
        far = cat(far, swap(far, 4))
        return cat(gather_quad(near), gather_quad(far))

    def swap_middle(v):
        rows = v.shape[0] // n
        out, at = [], 0
        for length in (8 * rows, v.shape[0] - 8 * rows):
            q = length // 4
            out += [v[at + i * q : at + (i + 1) * q] for i in (0, 2, 1, 3)]
            at += length
        return cat(*out)

    def scatter_quad(v):
        h = v.shape[0] // 2
        v = add(v[:h], swap(v[h:], 2, 1))
        h //= 2
        return add(v[:h], swap(v[h:], 1, 2))

    def scatter(v):
        rows = v.shape[0] // n
        far = scatter_quad(v[8 * rows :])
        near = scatter_quad(v[: 8 * rows])
        h = far.shape[0] // 2
        far = add(far[:h], swap(far[h:], 4))
        near = add(near[:rows], swap(near[rows:], 4))
        v = cat(near, far)
        for bit in reversed(long_bits):
            h = v.shape[0] // 2
            got = swap(v[h:], bit)
            v = add(v[:h], got) if h > rows else v[:h].astype(F32) + got.astype(F32)
        return v

    def sum_sections(v):
        for bit in [1 << i for i in range(n.bit_length() - 1)]:
            v = v + swap(v, bit)
        return v

    def tp_swap(v):
        return lax.ppermute(v, "tp", [(t, t ^ 1) for t in range(tp)])

    def tp_sum(v):
        if tp == 2:
            return v.astype(F32) + swap_middle(tp_swap(v)).astype(F32)
        t = lax.axis_index("tp") % 2
        both = lax.psum(jnp.stack([jnp.where(t == 0, v, 0), jnp.where(t == 1, v, 0)]), "tp").astype(F32)
        mine = jnp.where(t == 0, both[0], both[1])
        return mine + swap_middle(jnp.where(t == 0, both[1], both[0]))

    def shards(preview, row_owner, norm_gain, w_gate, w_up, w_down, score_vec):
        width = preview.shape[1]
        dims = (((1,), (1,)), ((), ()))
        owner_lanes = jnp.broadcast_to(row_owner.astype(BF16)[:, None], (row_owner.shape[0], LANES))
        both = gather(jnp.concatenate([preview, owner_lanes], axis=1))
        rows_all = both[:, :width].astype(F32)
        owner = both[:, width].astype(jnp.int32)
        member = (owner[:, None] == jnp.arange(CAND, dtype=jnp.int32)[None, :]).astype(F32)
        x = (rows_all * norm_gain[None, :]).astype(BF16)
        sq = tp_sum(jnp.sum(rows_all * rows_all, axis=1)[:, None])
        scale = lax.rsqrt(sq / (width * tp) + 1e-05)
        units = w_gate.shape[0]
        gate = lax.dot_general(x, w_gate, dims, preferred_element_type=F32).astype(BF16)
        up = lax.dot_general(x, w_up, dims, preferred_element_type=F32).astype(BF16)
        gate_up = tp_sum(jnp.concatenate([gate, up], axis=1)) * scale
        hidden = (jax.nn.silu(gate_up[:, :units]) * gate_up[:, units:]).astype(BF16)
        unit_score = jnp.sum(w_down.astype(F32) * score_vec[None, :], axis=1)
        rows = preview.shape[0]
        row_part = jnp.sum(hidden.astype(F32) * unit_score[None, :], axis=1)
        own_part = jnp.sum(preview.astype(F32) * score_vec[None, :], axis=1)
        totals = jnp.sum(member * row_part[:, None], axis=0) + jnp.sum(member[:rows] * own_part[:, None], axis=0)
        totals = tp_swap(totals) + totals if tp == 2 else lax.psum(totals, "tp")
        totals = sum_sections(totals)
        scores = totals / jnp.sum(member, axis=0)
        down = jnp.dot(hidden, w_down, preferred_element_type=F32).astype(BF16)
        verified = (preview.astype(F32) + scatter(down)).astype(BF16)
        return verified, scores

    return shards


NT = (((1,), (1,)), ((), ()))
VMEM = pl.BlockSpec(memory_space=pltpu.VMEM)
TILE = 256


def call(body, out_shape, args, scratch, megabytes, flops):
    size = sum(a.size * a.dtype.itemsize for a in args)
    return pl.pallas_call(
        body,
        out_shape=out_shape,
        in_specs=[VMEM] * len(args),
        out_specs=jax.tree.map(lambda _: VMEM, out_shape),
        scratch_shapes=scratch,
        compiler_params=pltpu.CompilerParams(vmem_limit_bytes=megabytes << 20),
        cost_estimate=pl.CostEstimate(flops=flops, bytes_accessed=size, transcendentals=0),
    )(*args)


def payload(preview, row_owner, flops):
    rows, width = preview.shape

    def body(rows_ref, owner_ref, out):
        out[:, :width] = rows_ref[...]
        at = lax.broadcasted_iota(jnp.int32, (rows, LANES), 0)
        owner = jnp.zeros((rows, LANES), F32)
        for i in range(rows):
            owner = jnp.where(at == i, owner_ref[i].astype(F32), owner)
        out[:, width:] = owner.astype(BF16)

    return pl.pallas_call(
        body,
        out_shape=jax.ShapeDtypeStruct((rows, width + LANES), BF16),
        in_specs=[VMEM, pl.BlockSpec(memory_space=pltpu.SMEM)],
        out_specs=VMEM,
        cost_estimate=pl.CostEstimate(flops=flops, bytes_accessed=4 * rows * width, transcendentals=0),
    )(preview, row_owner)


def join(a, b, flops):
    def body(a_ref, b_ref, out):
        out[: a.shape[0], :] = a_ref[...]
        out[a.shape[0] :, :] = b_ref[...]

    return call(body, jax.ShapeDtypeStruct((a.shape[0] + b.shape[0], a.shape[1]), a.dtype), (a, b), [], 4, flops)


def gate_up(pieces, places, gain, w_gate, w_up):
    rows, width = sum(p.shape[0] for p in pieces), gain.shape[1]
    units = w_gate.shape[0]
    half = rows // 2

    def body(*refs):
        given = refs[: len(pieces)]
        gain_ref, gate_ref, up_ref, near, far, squares, owner, x = refs[len(pieces) :]
        for ref, blocks in zip(given, places):
            size = ref.shape[0] // len(blocks)
            for i, to in enumerate(blocks):
                v = ref[i * size : (i + 1) * size, :width].astype(F32)
                here = slice(to, to + size)
                owner[here, :] = ref[i * size : (i + 1) * size, width:].astype(F32)
                squares[here, :] = jnp.broadcast_to(jnp.sum(v * v, axis=1, keepdims=True), (size, LANES))
                x[here, :] = (v * gain_ref[...]).astype(BF16)

        @pl.loop(0, units // TILE)
        def _(i):
            tile = pl.ds(pl.multiple_of(i * TILE, TILE), TILE)
            for k, w in enumerate((gate_ref, up_ref)):
                product = lax.dot_general(x[...], w[tile, :], NT, preferred_element_type=F32).astype(BF16)
                near[k, :, tile] = product[:half]
                far[k, :, tile] = product[half:]

    part = jax.ShapeDtypeStruct((2, half, units), BF16)
    lanes = jax.ShapeDtypeStruct((rows, LANES), F32)
    out_shape = (part, part, lanes, lanes)
    scratch = [pltpu.VMEM((rows, width), BF16)]
    return call(body, out_shape, (*pieces, gain, w_gate, w_up), scratch, 12, 4 * rows * width * units)


def down_rows(first, mine, theirs, squares, other_squares, owner, w_down, score, own, devices, flops):
    units, width = w_down.shape
    rows = squares.shape[0] // 2
    q = rows // 4
    wide = 2048

    def body(a, b, sq, other_sq, owner_ref, w, score_ref, own_ref, down, totals, hidden):
        for block, other in enumerate((0, 2, 1, 3)):
            here = slice(block * q, (block + 1) * q)
            there = slice(other * q, (other + 1) * q)
            both = sq[first + block * q : first + (block + 1) * q, :1]
            both += other_sq[first + other * q : first + (other + 1) * q, :1]
            scale = lax.rsqrt(both / (2 * width) + 1e-05)
            for lo in range(0, units, TILE):
                cols = slice(lo, lo + TILE)
                g = (a[0, here, cols].astype(F32) + b[0, there, cols].astype(F32)) * scale
                u = (a[1, here, cols].astype(F32) + b[1, there, cols].astype(F32)) * scale
                hidden[here, cols] = (jax.nn.silu(g) * u).astype(BF16)
        row_part = jnp.zeros((rows, 1), F32)
        for lo in range(0, width, wide):
            cols = slice(lo, lo + wide)
            product = jnp.dot(hidden[...], w[:, cols], preferred_element_type=F32)
            down[:, cols] = product.astype(BF16)
            row_part += jnp.sum(product * score_ref[:, cols], axis=1, keepdims=True)
        group = owner_ref[first : first + rows, :]
        member = group == lax.broadcasted_iota(jnp.int32, group.shape, 1).astype(F32)
        total = jnp.sum(jnp.where(member, row_part, 0.0), axis=0, keepdims=True)
        if first == 0:
            h = own_ref.shape[0]
            own_part = jnp.sum(own_ref[:, :width].astype(F32) * score_ref[...], axis=1, keepdims=True)
            total += jnp.sum(jnp.where(member[:h], own_part, 0.0), axis=0, keepdims=True)
        totals[...] = jnp.zeros_like(totals)
        totals[0:1, :] = total
        totals[1:2, :] = jnp.sum(member.astype(F32), axis=0, keepdims=True) / devices

    out_shape = (jax.ShapeDtypeStruct((rows, width), BF16), jax.ShapeDtypeStruct((8, LANES), F32))
    args = (mine, theirs, squares, other_squares, owner, w_down, score, own)
    return call(body, out_shape, args, [pltpu.VMEM((rows, units), BF16)], 12, flops)


def paired(n, tp):
    def swap(v, even, odd=None):
        odd = even if odd is None else odd
        pairs = [(s * tp + t, (s ^ (odd if t else even)) * tp + t) for s in range(n) for t in range(tp)]
        return lax.ppermute(v, BOTH, pairs)

    def tp_swap(v):
        return lax.ppermute(v, "tp", [(0, 1), (1, 0)])

    after = lax.optimization_barrier

    def shards(preview, row_owner, norm_gain, w_gate, w_up, w_down, score_vec):
        rows = preview.shape[0]
        own = payload(preview, row_owner, 10**10)
        z2, z1 = swap(own, 8), swap(own, 4)
        z3 = swap(z2, 4)
        near = join(own, z1, 10**10)
        near_a, near_b = swap(near, 1, 2), swap(near, 2, 1)
        far = join(z2, z3, 10**10)
        far_a, far_b = swap(far, 1, 2), swap(far, 2, 1)
        near_a, near_b = after((near_a, near_b))
        near_c = swap(near_a, 2, 1)
        far_a, far_b = after((far_a, far_b))
        far_c = swap(far_a, 2, 1)
        pieces = [near, near_a, near_b, near_c, far, far_a, far_b, far_c]
        q = near.shape[0]
        places = [(i * q,) for i in range(len(pieces))]
        half = 4 * q
        gain, score = norm_gain[None, :], score_vec[None, :]
        part_near, part_far, squares, owner = gate_up(pieces, places, gain, w_gate, w_up)
        other_squares, other_far, other_near = tp_swap(squares), tp_swap(part_far), tp_swap(part_near)

        def down(first, mine, other, flops):
            return down_rows(first, mine, other, squares, other_squares, owner, w_down, score, own, n * tp, flops)

        f, totals_far = down(half, part_far, other_far, 10**9)
        f, part_near = after((f, part_near))
        g, totals_near = down(0, part_near, other_near, 10**10)
        f3, f2 = swap(f[3 * q :], 2, 1), swap(f[2 * q : 3 * q], 2, 1)
        totals = totals_far + totals_near
        f3, g, t = after((f3, g, tp_swap(totals)))
        totals = totals + t
        f1 = swap(add(f[q : 2 * q], f3), 1, 2)
        g3, g2 = swap(g[3 * q :], 2, 1), swap(g[2 * q : 3 * q], 2, 1)
        f1, f2, t = after((f1, f2, swap(totals, 1)))
        totals = totals + t
        f = (f[:q].astype(F32) + f2.astype(F32) + f1.astype(F32)).astype(BF16)
        z3 = swap(f[rows:], 4)
        g3, t = after((g3, swap(totals, 2)))
        totals = totals + t
        g1 = swap(add(g[q : 2 * q], g3), 1, 2)
        z3, totals = after((z3, totals))
        z2 = swap(add(f[:rows], z3), 8)
        g1, g2, t = after((g1, g2, swap(totals, 4)))
        totals = totals + t
        g = g[:q].astype(F32) + g2.astype(F32) + g1.astype(F32)
        z1 = swap(g[rows:].astype(BF16), 4)
        totals = totals + swap(totals, 8)
        verified = (own[:, : preview.shape[1]].astype(F32) + g[:rows] + z1.astype(F32) + z2.astype(F32)).astype(BF16)
        return verified, totals[0, :CAND] / totals[1, :CAND]

    return shards


def solution(mesh):
    n, tp = mesh.shape["section"], mesh.shape["tp"]
    placed = (
        P("section", "tp"),
        P("section"),
        P("tp"),
        P("section", "tp"),
        P("section", "tp"),
        P("section", "tp"),
        P("tp"),
    )
    return jax.shard_map(
        (paired if (n, tp) == (16, 2) else general)(n, tp),
        mesh=mesh,
        in_specs=placed,
        out_specs=(P("section", "tp"), P()),
        check_vma=False,
    )
```

```python
import jax
import jax.numpy as jnp
from jax import lax
from jax.experimental import pallas as pl
from jax.experimental.pallas import tpu as pltpu
from jax.sharding import PartitionSpec as P

CAND = 32
LANES = 128
BOTH = ("section", "tp")
F32 = jnp.float32
BF16 = jnp.bfloat16


def cat(*parts):
    return jnp.concatenate(parts, axis=0)


def add(a, b):
    return (a.astype(F32) + b.astype(F32)).astype(BF16)


def general(n, tp):
    def swap(v, even, odd=None):
        odd = even if odd is None else odd
        pairs = [(s * tp + t, (s ^ (odd if t % 2 else even)) * tp + t) for s in range(n) for t in range(tp)]
        return lax.ppermute(v, BOTH, pairs)

    long_bits = [8 << i for i in range((n // 8).bit_length() - 1)]

    def gather_quad(g):
        a = swap(g, 1, 2)
        g = cat(g, a)
        return cat(g, swap(g, 2, 1))

    def gather(own):
        rows = own.shape[0]
        far = own
        for bit in long_bits:
            far = cat(far, swap(far, bit))
        far = far[rows:]
        near = cat(own, swap(own, 4))
        far = cat(far, swap(far, 4))
        return cat(gather_quad(near), gather_quad(far))

    def swap_middle(v):
        rows = v.shape[0] // n
        out, at = [], 0
        for length in (8 * rows, v.shape[0] - 8 * rows):
            q = length // 4
            out += [v[at + i * q : at + (i + 1) * q] for i in (0, 2, 1, 3)]
            at += length
        return cat(*out)

    def scatter_quad(v):
        h = v.shape[0] // 2
        v = add(v[:h], swap(v[h:], 2, 1))
        h //= 2
        return add(v[:h], swap(v[h:], 1, 2))

    def scatter(v):
        rows = v.shape[0] // n
        far = scatter_quad(v[8 * rows :])
        near = scatter_quad(v[: 8 * rows])
        h = far.shape[0] // 2
        far = add(far[:h], swap(far[h:], 4))
        near = add(near[:rows], swap(near[rows:], 4))
        v = cat(near, far)
        for bit in reversed(long_bits):
            h = v.shape[0] // 2
            got = swap(v[h:], bit)
            v = add(v[:h], got) if h > rows else v[:h].astype(F32) + got.astype(F32)
        return v

    def sum_sections(v):
        for bit in [1 << i for i in range(n.bit_length() - 1)]:
            v = v + swap(v, bit)
        return v

    def tp_swap(v):
        return lax.ppermute(v, "tp", [(t, t ^ 1) for t in range(tp)])

    def tp_sum(v):
        if tp == 2:
            return v.astype(F32) + swap_middle(tp_swap(v)).astype(F32)
        t = lax.axis_index("tp") % 2
        both = lax.psum(jnp.stack([jnp.where(t == 0, v, 0), jnp.where(t == 1, v, 0)]), "tp").astype(F32)
        mine = jnp.where(t == 0, both[0], both[1])
        return mine + swap_middle(jnp.where(t == 0, both[1], both[0]))

    def shards(preview, row_owner, norm_gain, w_gate, w_up, w_down, score_vec):
        width = preview.shape[1]
        dims = (((1,), (1,)), ((), ()))
        owner_lanes = jnp.broadcast_to(row_owner.astype(BF16)[:, None], (row_owner.shape[0], LANES))
        both = gather(jnp.concatenate([preview, owner_lanes], axis=1))
        rows_all = both[:, :width].astype(F32)
        owner = both[:, width].astype(jnp.int32)
        member = (owner[:, None] == jnp.arange(CAND, dtype=jnp.int32)[None, :]).astype(F32)
        x = (rows_all * norm_gain[None, :]).astype(BF16)
        sq = tp_sum(jnp.sum(rows_all * rows_all, axis=1)[:, None])
        scale = lax.rsqrt(sq / (width * tp) + 1e-05)
        units = w_gate.shape[0]
        gate = lax.dot_general(x, w_gate, dims, preferred_element_type=F32).astype(BF16)
        up = lax.dot_general(x, w_up, dims, preferred_element_type=F32).astype(BF16)
        gate_up = tp_sum(jnp.concatenate([gate, up], axis=1)) * scale
        hidden = (jax.nn.silu(gate_up[:, :units]) * gate_up[:, units:]).astype(BF16)
        unit_score = jnp.sum(w_down.astype(F32) * score_vec[None, :], axis=1)
        rows = preview.shape[0]
        row_part = jnp.sum(hidden.astype(F32) * unit_score[None, :], axis=1)
        own_part = jnp.sum(preview.astype(F32) * score_vec[None, :], axis=1)
        totals = jnp.sum(member * row_part[:, None], axis=0) + jnp.sum(member[:rows] * own_part[:, None], axis=0)
        totals = tp_swap(totals) + totals if tp == 2 else lax.psum(totals, "tp")
        totals = sum_sections(totals)
        scores = totals / jnp.sum(member, axis=0)
        down = jnp.dot(hidden, w_down, preferred_element_type=F32).astype(BF16)
        verified = (preview.astype(F32) + scatter(down)).astype(BF16)
        return verified, scores

    return shards


NT = (((1,), (1,)), ((), ()))
VMEM = pl.BlockSpec(memory_space=pltpu.VMEM)
TILE = 256


def call(body, out_shape, args, scratch, megabytes, flops):
    size = sum(a.size * a.dtype.itemsize for a in args)
    return pl.pallas_call(
        body,
        out_shape=out_shape,
        in_specs=[VMEM] * len(args),
        out_specs=jax.tree.map(lambda _: VMEM, out_shape),
        scratch_shapes=scratch,
        compiler_params=pltpu.CompilerParams(vmem_limit_bytes=megabytes << 20),
        cost_estimate=pl.CostEstimate(flops=flops, bytes_accessed=size, transcendentals=0),
    )(*args)


def payload(preview, row_owner, flops):
    rows, width = preview.shape

    def body(rows_ref, owner_ref, out):
        out[:, :width] = rows_ref[...]
        at = lax.broadcasted_iota(jnp.int32, (rows, LANES), 0)
        owner = jnp.zeros((rows, LANES), F32)
        for i in range(rows):
            owner = jnp.where(at == i, owner_ref[i].astype(F32), owner)
        out[:, width:] = owner.astype(BF16)

    return pl.pallas_call(
        body,
        out_shape=jax.ShapeDtypeStruct((rows, width + LANES), BF16),
        in_specs=[VMEM, pl.BlockSpec(memory_space=pltpu.SMEM)],
        out_specs=VMEM,
        cost_estimate=pl.CostEstimate(flops=flops, bytes_accessed=4 * rows * width, transcendentals=0),
    )(preview, row_owner)


def join(arrays, flops):
    rows = sum(a.shape[0] for a in arrays)

    def body(*refs):
        at = 0
        for ref in refs[:-1]:
            refs[-1][at : at + ref.shape[0], :] = ref[...]
            at += ref.shape[0]

    return call(body, jax.ShapeDtypeStruct((rows, arrays[0].shape[1]), arrays[0].dtype), arrays, [], 4, flops)


def gate_up(pieces, places, gain, w_gate, w_up):
    rows, width = sum(p.shape[0] for p in pieces), gain.shape[1]
    units = w_gate.shape[0]

    def body(*refs):
        given = refs[: len(pieces)]
        gain_ref, gate_ref, up_ref, part, squares, owner, x = refs[len(pieces) :]
        for ref, blocks in zip(given, places):
            size = ref.shape[0] // len(blocks)
            for i, to in enumerate(blocks):
                v = ref[i * size : (i + 1) * size, :width].astype(F32)
                here = slice(to, to + size)
                owner[here, :] = ref[i * size : (i + 1) * size, width:].astype(F32)
                squares[here, :] = jnp.broadcast_to(jnp.sum(v * v, axis=1, keepdims=True), (size, LANES))
                x[here, :] = (v * gain_ref[...]).astype(BF16)

        @pl.loop(0, units // TILE)
        def _(i):
            tile = pl.ds(pl.multiple_of(i * TILE, TILE), TILE)
            for k, w in enumerate((gate_ref, up_ref)):
                part[k, :, tile] = lax.dot_general(x[...], w[tile, :], NT, preferred_element_type=F32).astype(BF16)

    lanes = jax.ShapeDtypeStruct((rows, LANES), F32)
    out_shape = (jax.ShapeDtypeStruct((2, rows, units), BF16), lanes, lanes)
    scratch = [pltpu.VMEM((rows, width), BF16)]
    return call(body, out_shape, (*pieces, gain, w_gate, w_up), scratch, 12, 4 * rows * width * units)


def split_lanes(total, rows):
    high = total.astype(BF16).astype(F32)
    middle = (total - high).astype(BF16).astype(F32)
    low = total - high - middle
    at = lax.broadcasted_iota(jnp.int32, (rows, LANES), 0)
    return jnp.where(at == 0, high, jnp.where(at == 1, middle, jnp.where(at == 2, low, 0.0))).astype(BF16)


def down_rows(mine, theirs, squares, other_squares, owner, w_down, score, own):
    units, width = w_down.shape
    rows = squares.shape[0]
    q = rows // 8
    h = q // 2
    wide = 1024

    def body(a, b, sq, other_sq, owner_ref, w, score_ref, own_ref, *rest):
        near, across, far, (totals, hidden) = rest[:4], rest[4], rest[5:9], rest[9:]
        for block in range(8):
            other = block ^ 3 if block % 4 in (1, 2) else block
            here = slice(block * q, (block + 1) * q)
            there = slice(other * q, (other + 1) * q)
            scale = lax.rsqrt((sq[here, :1] + other_sq[there, :1]) / (2 * width) + 1e-05)
            for lo in range(0, units, TILE):
                cols = slice(lo, lo + TILE)
                g = (a[0, here, cols].astype(F32) + b[0, there, cols].astype(F32)) * scale
                u = (a[1, here, cols].astype(F32) + b[1, there, cols].astype(F32)) * scale
                hidden[here, cols] = (jax.nn.silu(g) * u).astype(BF16)
        row_part = jnp.zeros((rows, 1), F32)
        for lo in range(0, width, wide):
            cols = slice(lo, lo + wide)
            product = jnp.dot(hidden[...], w[:, cols], preferred_element_type=F32)
            product_bf16 = product.astype(BF16)
            for block in range(4):
                at = block * q
                near[block][:, cols] = product_bf16[at : at + h]
                across[block * h : (block + 1) * h, cols] = product_bf16[at + h : at + q]
                far[block][:, cols] = product_bf16[4 * q + at : 5 * q + at]
            row_part += jnp.sum(product * score_ref[:, cols], axis=1, keepdims=True)
        group = owner_ref[...]
        member = group == lax.broadcasted_iota(jnp.int32, group.shape, 1).astype(F32)
        total = jnp.sum(jnp.where(member, row_part, 0.0), axis=0, keepdims=True)
        own_part = jnp.sum(own_ref[:, :width].astype(F32) * score_ref[...], axis=1, keepdims=True)
        total += jnp.sum(jnp.where(member[:h], own_part, 0.0), axis=0, keepdims=True)
        totals[...] = jnp.zeros_like(totals)
        totals[0:1, :] = total
        totals[1:2, :] = jnp.sum(member.astype(F32), axis=0, keepdims=True)
        far[3][:, width:] = split_lanes(total, q)

    shapes = [(h, width)] * 4 + [(4 * h, width)] + [(q, width)] * 3 + [(q, width + LANES)]
    blocks = [jax.ShapeDtypeStruct(shape, BF16) for shape in shapes]
    out_shape = (*blocks, jax.ShapeDtypeStruct((8, LANES), F32))
    args = (mine, theirs, squares, other_squares, owner, w_down, score, own)
    return call(body, out_shape, args, [pltpu.VMEM((rows, units), BF16)], 14, 2 * rows * units * width)


def carried(ref):
    return sum(ref[i : i + 1, ref.shape[1] - LANES :].astype(F32) for i in range(3))


def fold(terms, totals, carriers, cuts, width):
    rows = terms[0].shape[0]
    count = len(terms)

    def body(*refs):
        given, totals_ref, brought = refs[:count], refs[count], refs[count + 1 : count + 1 + len(carriers)]
        outs, totals_out = refs[count + 1 + len(carriers) : -1], refs[-1]
        total = totals_ref[0:1, :]
        for ref in brought:
            total += carried(ref)
        totals_out[...] = totals_ref[...]
        totals_out[0:1, :] = total
        for (start, stop, sent), out in zip(cuts, outs):
            for lo in range(start, stop, 16):
                here = slice(lo, lo + 16)
                v = given[0][here, :width].astype(F32)
                for ref in given[1:]:
                    v += ref[here, :width].astype(F32)
                out[lo - start : lo - start + 16, :width] = v.astype(BF16)
            if sent:
                out[:, width:] = split_lanes(total, stop - start)

    shapes = [jax.ShapeDtypeStruct((stop - start, width + (LANES if sent else 0)), BF16) for start, stop, sent in cuts]
    out_shape = (*shapes, jax.ShapeDtypeStruct(totals.shape, F32))
    return call(body, out_shape, (*terms, totals, *carriers), [], 8, 2 * rows * width * count)


def paired(n, tp):
    def swap(v, even, odd=None):
        odd = even if odd is None else odd
        pairs = [(s * tp + t, (s ^ (odd if t else even)) * tp + t) for s in range(n) for t in range(tp)]
        return lax.ppermute(v, BOTH, pairs)

    def tp_swap(v):
        return lax.ppermute(v, "tp", [(0, 1), (1, 0)])

    after = lax.optimization_barrier

    def shards(preview, row_owner, norm_gain, w_gate, w_up, w_down, score_vec):
        rows = preview.shape[0]
        own = payload(preview, row_owner, 10**10)
        z2, z1 = swap(own, 8), swap(own, 4)
        own_a, own_b = swap(own, 1, 2), swap(own, 2, 1)
        z3 = swap(z2, 4)
        pair = join((z1, z2), 10**10)
        pair_a, pair_b = swap(pair, 1, 2), swap(pair, 2, 1)
        own_a, own_b, pair = after((own_a, own_b, pair))
        own_c = swap(own_a, 2, 1)
        z3 = join((z3,), 10**10)
        z3_a, z3_b = swap(z3, 1, 2), swap(z3, 2, 1)
        pair_a = join((pair_a,), 10**10)
        pair_c = swap(pair_a, 2, 1)
        z3_c = swap(z3_a, 2, 1)

        q, half = 2 * rows, 8 * rows
        pieces, places = [], []
        triples = ((own, pair, z3), (own_a, pair_a, z3_a), (own_b, pair_b, z3_b), (own_c, pair_c, z3_c))
        for i, triple in enumerate(triples):
            at = q * i
            pieces += triple
            places += [(at,), (at + rows, half + at), (half + at + rows,)]
        gain, score = norm_gain[None, :], score_vec[None, :]
        part, squares, owner = gate_up(pieces, places, gain, w_gate, w_up)
        other, other_squares = tp_swap(part), tp_swap(squares)
        *near, across, f0, f1, f2, f3, totals = down_rows(part, other, squares, other_squares, owner, w_down, score, own)
        width = preview.shape[1]
        counts = totals[1, :CAND]
        f3 = swap(f3, 2, 1)
        across = swap(across, 4)
        f2 = swap(f2, 2, 1)
        send, totals = fold([f1, f3], totals, [f3], [(0, q, True)], width)
        f1 = swap(send, 1, 2)
        keep, send, totals = fold([f0, f1, f2], totals, [f1], [(0, rows, False), (rows, q, True)], width)
        z3 = swap(send, 4)
        near = [add(v, across[i * rows : (i + 1) * rows]) for i, v in enumerate(near)]
        n3, n2 = swap(near[3], 2, 1), swap(near[2], 2, 1)
        send, totals = fold([keep, z3], totals, [z3], [(0, rows, True)], width)
        z2 = swap(send, 8)
        n1 = swap(add(near[1], n3), 1, 2)
        total = totals[0, :] + jnp.sum(z2[:3, width:].astype(F32), axis=0)
        total = total + tp_swap(total)
        verified = own[:, :width].astype(F32) + near[0].astype(F32)
        verified = verified + n2.astype(F32) + n1.astype(F32) + z2[:, :width].astype(F32)
        return verified.astype(BF16), total[:CAND] / counts

    return shards


def solution(mesh):
    n, tp = mesh.shape["section"], mesh.shape["tp"]
    placed = (
        P("section", "tp"),
        P("section"),
        P("tp"),
        P("section", "tp"),
        P("section", "tp"),
        P("section", "tp"),
        P("tp"),
    )
    return jax.shard_map(
        (paired if (n, tp) == (16, 2) else general)(n, tp),
        mesh=mesh,
        in_specs=placed,
        out_specs=(P("section", "tp"), P()),
        check_vma=False,
    )
```

```python
import jax
import jax.numpy as jnp
from jax import lax
from jax.experimental import pallas as pl
from jax.experimental.pallas import tpu as pltpu
from jax.sharding import PartitionSpec as P

CAND = 32
LANES = 128
BOTH = ("section", "tp")
F32 = jnp.float32
BF16 = jnp.bfloat16


def cat(*parts):
    return jnp.concatenate(parts, axis=0)


def add(a, b):
    return (a.astype(F32) + b.astype(F32)).astype(BF16)


def general(n, tp):
    def swap(v, even, odd=None):
        odd = even if odd is None else odd
        pairs = [(s * tp + t, (s ^ (odd if t % 2 else even)) * tp + t) for s in range(n) for t in range(tp)]
        return lax.ppermute(v, BOTH, pairs)

    long_bits = [8 << i for i in range((n // 8).bit_length() - 1)]

    def gather_quad(g):
        a = swap(g, 1, 2)
        g = cat(g, a)
        return cat(g, swap(g, 2, 1))

    def gather(own):
        rows = own.shape[0]
        far = own
        for bit in long_bits:
            far = cat(far, swap(far, bit))
        far = far[rows:]
        near = cat(own, swap(own, 4))
        far = cat(far, swap(far, 4))
        return cat(gather_quad(near), gather_quad(far))

    def swap_middle(v):
        rows = v.shape[0] // n
        out, at = [], 0
        for length in (8 * rows, v.shape[0] - 8 * rows):
            q = length // 4
            out += [v[at + i * q : at + (i + 1) * q] for i in (0, 2, 1, 3)]
            at += length
        return cat(*out)

    def scatter_quad(v):
        h = v.shape[0] // 2
        v = add(v[:h], swap(v[h:], 2, 1))
        h //= 2
        return add(v[:h], swap(v[h:], 1, 2))

    def scatter(v):
        rows = v.shape[0] // n
        far = scatter_quad(v[8 * rows :])
        near = scatter_quad(v[: 8 * rows])
        h = far.shape[0] // 2
        far = add(far[:h], swap(far[h:], 4))
        near = add(near[:rows], swap(near[rows:], 4))
        v = cat(near, far)
        for bit in reversed(long_bits):
            h = v.shape[0] // 2
            got = swap(v[h:], bit)
            v = add(v[:h], got) if h > rows else v[:h].astype(F32) + got.astype(F32)
        return v

    def sum_sections(v):
        for bit in [1 << i for i in range(n.bit_length() - 1)]:
            v = v + swap(v, bit)
        return v

    def tp_swap(v):
        return lax.ppermute(v, "tp", [(t, t ^ 1) for t in range(tp)])

    def tp_sum(v):
        if tp == 2:
            return v.astype(F32) + swap_middle(tp_swap(v)).astype(F32)
        t = lax.axis_index("tp") % 2
        both = lax.psum(jnp.stack([jnp.where(t == 0, v, 0), jnp.where(t == 1, v, 0)]), "tp").astype(F32)
        mine = jnp.where(t == 0, both[0], both[1])
        return mine + swap_middle(jnp.where(t == 0, both[1], both[0]))

    def shards(preview, row_owner, norm_gain, w_gate, w_up, w_down, score_vec):
        width = preview.shape[1]
        dims = (((1,), (1,)), ((), ()))
        owner_lanes = jnp.broadcast_to(row_owner.astype(BF16)[:, None], (row_owner.shape[0], LANES))
        both = gather(jnp.concatenate([preview, owner_lanes], axis=1))
        rows_all = both[:, :width].astype(F32)
        owner = both[:, width].astype(jnp.int32)
        member = (owner[:, None] == jnp.arange(CAND, dtype=jnp.int32)[None, :]).astype(F32)
        x = (rows_all * norm_gain[None, :]).astype(BF16)
        sq = tp_sum(jnp.sum(rows_all * rows_all, axis=1)[:, None])
        scale = lax.rsqrt(sq / (width * tp) + 1e-05)
        units = w_gate.shape[0]
        gate = lax.dot_general(x, w_gate, dims, preferred_element_type=F32).astype(BF16)
        up = lax.dot_general(x, w_up, dims, preferred_element_type=F32).astype(BF16)
        gate_up = tp_sum(jnp.concatenate([gate, up], axis=1)) * scale
        hidden = (jax.nn.silu(gate_up[:, :units]) * gate_up[:, units:]).astype(BF16)
        unit_score = jnp.sum(w_down.astype(F32) * score_vec[None, :], axis=1)
        rows = preview.shape[0]
        row_part = jnp.sum(hidden.astype(F32) * unit_score[None, :], axis=1)
        own_part = jnp.sum(preview.astype(F32) * score_vec[None, :], axis=1)
        totals = jnp.sum(member * row_part[:, None], axis=0) + jnp.sum(member[:rows] * own_part[:, None], axis=0)
        totals = tp_swap(totals) + totals if tp == 2 else lax.psum(totals, "tp")
        totals = sum_sections(totals)
        scores = totals / jnp.sum(member, axis=0)
        down = jnp.dot(hidden, w_down, preferred_element_type=F32).astype(BF16)
        verified = (preview.astype(F32) + scatter(down)).astype(BF16)
        return verified, scores

    return shards


NT = (((1,), (1,)), ((), ()))
VMEM = pl.BlockSpec(memory_space=pltpu.VMEM)
TILE = 256


def call(body, out_shape, args, scratch, megabytes, flops):
    size = sum(a.size * a.dtype.itemsize for a in args)
    return pl.pallas_call(
        body,
        out_shape=out_shape,
        in_specs=[VMEM] * len(args),
        out_specs=jax.tree.map(lambda _: VMEM, out_shape),
        scratch_shapes=scratch,
        compiler_params=pltpu.CompilerParams(vmem_limit_bytes=megabytes << 20),
        cost_estimate=pl.CostEstimate(flops=flops, bytes_accessed=size, transcendentals=0),
    )(*args)


def payload(preview, row_owner, flops):
    rows, width = preview.shape

    def body(rows_ref, owner_ref, out):
        out[:, :width] = rows_ref[...]
        at = lax.broadcasted_iota(jnp.int32, (rows, LANES), 0)
        owner = jnp.zeros((rows, LANES), F32)
        for i in range(rows):
            owner = jnp.where(at == i, owner_ref[i].astype(F32), owner)
        out[:, width:] = owner.astype(BF16)

    return pl.pallas_call(
        body,
        out_shape=pltpu.VMEM((rows, width + LANES), BF16),
        in_specs=[VMEM, pl.BlockSpec(memory_space=pltpu.SMEM)],
        out_specs=VMEM,
        cost_estimate=pl.CostEstimate(flops=flops, bytes_accessed=4 * rows * width, transcendentals=0),
    )(preview, row_owner)


def join(arrays, flops):
    rows = sum(a.shape[0] for a in arrays)

    def body(*refs):
        at = 0
        for ref in refs[:-1]:
            refs[-1][at : at + ref.shape[0], :] = ref[...]
            at += ref.shape[0]

    return call(body, jax.ShapeDtypeStruct((rows, arrays[0].shape[1]), arrays[0].dtype), arrays, [], 4, flops)


def place_rows(pieces, places, gain_ref, x, squares, owner):
    width = x.shape[1]
    for ref, blocks in zip(pieces, places):
        size = ref.shape[0] // len(blocks)
        for i, to in enumerate(blocks):
            v = ref[i * size : (i + 1) * size, :width].astype(F32)
            here = slice(to, to + size)
            owner[here, :] = ref[i * size : (i + 1) * size, width:].astype(F32)
            squares[here, :] = jnp.broadcast_to(jnp.sum(v * v, axis=1, keepdims=True), (size, LANES))
            x[here, :] = (v * gain_ref[...]).astype(BF16)


def early_rows(pieces, places, gain, rows, flops):
    def body(*refs):
        place_rows(refs[: len(pieces)], places, *refs[len(pieces) :])

    lanes = jax.ShapeDtypeStruct((rows, LANES), F32)
    out_shape = (jax.ShapeDtypeStruct((rows, gain.shape[1]), BF16), lanes, lanes)
    return call(body, out_shape, (*pieces, gain), [], 4, flops)


def gate_up(early, early_places, pieces, places, gain, w_gate, w_up):
    rows, width = early[0].shape
    units = w_gate.shape[0]

    def body(x_in, squares_in, owner_in, *refs):
        given = refs[: len(pieces)]
        gain_ref, gate_ref, up_ref, part, squares, owner, x = refs[len(pieces) :]
        for start, stop in early_places:
            for source, to in ((x_in, x), (squares_in, squares), (owner_in, owner)):
                to[start:stop, :] = source[start:stop, :]
        place_rows(given, places, gain_ref, x, squares, owner)

        @pl.loop(0, units // TILE)
        def _(i):
            tile = pl.ds(pl.multiple_of(i * TILE, TILE), TILE)
            for k, w in enumerate((gate_ref, up_ref)):
                part[k, :, tile] = lax.dot_general(x[...], w[tile, :], NT, preferred_element_type=F32).astype(BF16)

    lanes = jax.ShapeDtypeStruct((rows, LANES), F32)
    out_shape = (jax.ShapeDtypeStruct((2, rows, units), BF16), lanes, lanes)
    scratch = [pltpu.VMEM((rows, width), BF16)]
    args = (*early, *pieces, gain, w_gate, w_up)
    return call(body, out_shape, args, scratch, 7, 4 * rows * width * units)


def split_lanes(total, rows):
    high = total.astype(BF16).astype(F32)
    middle = (total - high).astype(BF16).astype(F32)
    low = total - high - middle
    at = lax.broadcasted_iota(jnp.int32, (rows, LANES), 0)
    return jnp.where(at == 0, high, jnp.where(at == 1, middle, jnp.where(at == 2, low, 0.0))).astype(BF16)


def down_rows(mine, theirs, squares, other_squares, owner, w_down, score, own):
    units, width = w_down.shape
    rows = squares.shape[0]
    q = rows // 8
    h = q // 2
    wide = 1024

    def body(a, b, sq, other_sq, owner_ref, w, score_ref, own_ref, *rest):
        near, across, far, (totals, hidden) = rest[:4], rest[4], rest[5:9], rest[9:]
        for block in range(8):
            other = block ^ 3 if block % 4 in (1, 2) else block
            here = slice(block * q, (block + 1) * q)
            there = slice(other * q, (other + 1) * q)
            scale = lax.rsqrt((sq[here, :1] + other_sq[there, :1]) / (2 * width) + 1e-05)
            for lo in range(0, units, TILE):
                cols = slice(lo, lo + TILE)
                g = (a[0, here, cols].astype(F32) + b[0, there, cols].astype(F32)) * scale
                u = (a[1, here, cols].astype(F32) + b[1, there, cols].astype(F32)) * scale
                hidden[here, cols] = (jax.nn.silu(g) * u).astype(BF16)
        row_part = jnp.zeros((rows, 1), F32)
        for lo in range(0, width, wide):
            cols = slice(lo, lo + wide)
            product = jnp.dot(hidden[...], w[:, cols], preferred_element_type=F32)
            product_bf16 = product.astype(BF16)
            for block in range(4):
                at = block * q
                near[block][:, cols] = product_bf16[at : at + h]
                across[block * h : (block + 1) * h, cols] = product_bf16[at + h : at + q]
                far[block][:, cols] = product_bf16[4 * q + at : 5 * q + at]
            row_part += jnp.sum(product * score_ref[:, cols], axis=1, keepdims=True)
        group = owner_ref[...]
        member = group == lax.broadcasted_iota(jnp.int32, group.shape, 1).astype(F32)
        total = jnp.sum(jnp.where(member, row_part, 0.0), axis=0, keepdims=True)
        own_part = jnp.sum(own_ref[:, :width].astype(F32) * score_ref[...], axis=1, keepdims=True)
        total += jnp.sum(jnp.where(member[:h], own_part, 0.0), axis=0, keepdims=True)
        totals[...] = jnp.zeros_like(totals)
        totals[0:1, :] = total
        totals[1:2, :] = jnp.sum(member.astype(F32), axis=0, keepdims=True)
        far[3][:, width:] = split_lanes(total, q)

    shapes = [(h, width)] * 4 + [(4 * h, width)] + [(q, width)] * 3 + [(q, width + LANES)]
    blocks = [jax.ShapeDtypeStruct(shape, BF16) for shape in shapes]
    out_shape = (*blocks, jax.ShapeDtypeStruct((8, LANES), F32))
    args = (mine, theirs, squares, other_squares, owner, w_down, score, own)
    return call(body, out_shape, args, [pltpu.VMEM((rows, units), BF16)], 14, 2 * rows * units * width)


def carried(ref):
    return sum(ref[i : i + 1, ref.shape[1] - LANES :].astype(F32) for i in range(3))


def fold(terms, totals, carriers, cuts, width, flops=0):
    count = len(terms)

    def body(*refs):
        given, totals_ref, brought = refs[:count], refs[count], refs[count + 1 : count + 1 + len(carriers)]
        outs, totals_out = refs[count + 1 + len(carriers) : -1], refs[-1]
        total = totals_ref[0:1, :]
        for ref in brought:
            total += carried(ref)
        totals_out[...] = totals_ref[...]
        totals_out[0:1, :] = total
        for (start, stop, sent), out in zip(cuts, outs):
            for lo in range(start, stop, 16):
                here = slice(lo, lo + 16)
                v = given[0][here, :width].astype(F32)
                for ref in given[1:]:
                    v += ref[here, :width].astype(F32)
                out[lo - start : lo - start + 16, :width] = v.astype(BF16)
            if sent:
                out[:, width:] = split_lanes(total, stop - start)

    shapes = [jax.ShapeDtypeStruct((stop - start, width + (LANES if sent else 0)), BF16) for start, stop, sent in cuts]
    out_shape = (*shapes, jax.ShapeDtypeStruct(totals.shape, F32))
    return call(body, out_shape, (*terms, totals, *carriers), [], 8, flops)


def paired(n, tp):
    def swap(v, even, odd=None):
        odd = even if odd is None else odd
        pairs = [(s * tp + t, (s ^ (odd if t else even)) * tp + t) for s in range(n) for t in range(tp)]
        return lax.ppermute(v, BOTH, pairs)

    def tp_swap(v):
        return lax.ppermute(v, "tp", [(0, 1), (1, 0)])

    after = lax.optimization_barrier

    def shards(preview, row_owner, norm_gain, w_gate, w_up, w_down, score_vec):
        rows = preview.shape[0]
        own = payload(preview, row_owner, 10**10)
        z2 = swap(own, 8)
        own_a, own_b = swap(own, 1, 2), swap(own, 2, 1)
        z3 = swap(z2, 4)
        z2, own_a, own_b = after((join((z2,), 10**10), own_a, own_b))
        z2_a, z2_b = swap(z2, 1, 2), swap(z2, 2, 1)
        own_c = swap(own_a, 2, 1)
        across = swap(join((own, own_a, own_b), 0), 4)
        z3 = join((z3,), 10**10)
        z3_a, z3_b = swap(z3, 1, 2), swap(z3, 2, 1)
        z2_a = join((z2_a,), 10**10)
        z3_a, z3_b, z2_b, own_c = after((z3_a, z3_b, z2_b, own_c))
        across_c = swap(own_c, 4)
        far_c = swap(join((z2_a, z3_a), 0), 2, 1)

        q, half = 2 * rows, 8 * rows
        gain, score = norm_gain[None, :], score_vec[None, :]
        pieces = [own, own_a, own_b, own_c, across, z2, z2_a, z2_b, z3, z3_a, z3_b]
        places = [(i * q,) for i in range(4)] + [tuple(i * q + rows for i in range(3))]
        places += [(half + i * q,) for i in range(3)] + [(half + i * q + rows,) for i in range(3)]
        early = early_rows(pieces, places, gain, 2 * half, 10**9)
        early_places = [(0, half - rows), (half, half + 3 * q)]
        late_places = [(half - rows,), (half + 3 * q,)]
        part, squares, owner = gate_up(early, early_places, [across_c, far_c], late_places, gain, w_gate, w_up)
        other, other_squares = tp_swap(part), tp_swap(squares)
        *near, across, f0, f1, f2, f3, totals = down_rows(part, other, squares, other_squares, owner, w_down, score, own)
        width = preview.shape[1]
        counts = totals[1, :CAND]
        f3 = swap(f3, 2, 1)
        across = swap(across, 4)
        f2 = swap(f2, 2, 1)
        send, totals = fold([f1, f3], totals, [f3], [(0, q, True)], width, 2 * 10**9)
        f1 = swap(send, 1, 2)
        f0, _ = fold([f0, f2], totals, [], [(0, q, False)], width, 2 * 10**9)
        keep, send, totals = fold([f0, f1], totals, [f1], [(0, rows, False), (rows, q, True)], width)
        z3 = swap(send, 4)
        near = [add(v, across[i * rows : (i + 1) * rows]) for i, v in enumerate(near)]
        n3, n2 = swap(near[3], 2, 1), swap(near[2], 2, 1)
        send, totals = fold([keep, z3], totals, [z3], [(0, rows, True)], width)
        z2 = swap(send, 8)
        n1 = swap(add(near[1], n3), 1, 2)
        total = totals[0, :] + jnp.sum(z2[:3, width:].astype(F32), axis=0)
        total = total + tp_swap(total)
        verified = own[:, :width].astype(F32) + near[0].astype(F32)
        verified = verified + n2.astype(F32) + n1.astype(F32) + z2[:, :width].astype(F32)
        return verified.astype(BF16), total[:CAND] / counts

    return shards


def solution(mesh):
    n, tp = mesh.shape["section"], mesh.shape["tp"]
    placed = (
        P("section", "tp"),
        P("section"),
        P("tp"),
        P("section", "tp"),
        P("section", "tp"),
        P("section", "tp"),
        P("tp"),
    )
    return jax.shard_map(
        (paired if (n, tp) == (16, 2) else general)(n, tp),
        mesh=mesh,
        in_specs=placed,
        out_specs=(P("section", "tp"), P()),
        check_vma=False,
    )
```

```python
import jax
import jax.numpy as jnp
from jax import lax
from jax.experimental import pallas as pl
from jax.experimental.pallas import tpu as pltpu
from jax.sharding import PartitionSpec as P

CAND = 32
LANES = 128
BOTH = ("section", "tp")
F32 = jnp.float32
BF16 = jnp.bfloat16


def cat(*parts):
    return jnp.concatenate(parts, axis=0)


def add(a, b):
    return (a.astype(F32) + b.astype(F32)).astype(BF16)


def general(n, tp):
    def swap(v, even, odd=None):
        odd = even if odd is None else odd
        pairs = [(s * tp + t, (s ^ (odd if t % 2 else even)) * tp + t) for s in range(n) for t in range(tp)]
        return lax.ppermute(v, BOTH, pairs)

    long_bits = [8 << i for i in range((n // 8).bit_length() - 1)]

    def gather_quad(g):
        a = swap(g, 1, 2)
        g = cat(g, a)
        return cat(g, swap(g, 2, 1))

    def gather(own):
        rows = own.shape[0]
        far = own
        for bit in long_bits:
            far = cat(far, swap(far, bit))
        far = far[rows:]
        near = cat(own, swap(own, 4))
        far = cat(far, swap(far, 4))
        return cat(gather_quad(near), gather_quad(far))

    def swap_middle(v):
        rows = v.shape[0] // n
        out, at = [], 0
        for length in (8 * rows, v.shape[0] - 8 * rows):
            q = length // 4
            out += [v[at + i * q : at + (i + 1) * q] for i in (0, 2, 1, 3)]
            at += length
        return cat(*out)

    def scatter_quad(v):
        h = v.shape[0] // 2
        v = add(v[:h], swap(v[h:], 2, 1))
        h //= 2
        return add(v[:h], swap(v[h:], 1, 2))

    def scatter(v):
        rows = v.shape[0] // n
        far = scatter_quad(v[8 * rows :])
        near = scatter_quad(v[: 8 * rows])
        h = far.shape[0] // 2
        far = add(far[:h], swap(far[h:], 4))
        near = add(near[:rows], swap(near[rows:], 4))
        v = cat(near, far)
        for bit in reversed(long_bits):
            h = v.shape[0] // 2
            got = swap(v[h:], bit)
            v = add(v[:h], got) if h > rows else v[:h].astype(F32) + got.astype(F32)
        return v

    def sum_sections(v):
        for bit in [1 << i for i in range(n.bit_length() - 1)]:
            v = v + swap(v, bit)
        return v

    def tp_swap(v):
        return lax.ppermute(v, "tp", [(t, t ^ 1) for t in range(tp)])

    def tp_sum(v):
        if tp == 2:
            return v.astype(F32) + swap_middle(tp_swap(v)).astype(F32)
        t = lax.axis_index("tp") % 2
        both = lax.psum(jnp.stack([jnp.where(t == 0, v, 0), jnp.where(t == 1, v, 0)]), "tp").astype(F32)
        mine = jnp.where(t == 0, both[0], both[1])
        return mine + swap_middle(jnp.where(t == 0, both[1], both[0]))

    def shards(preview, row_owner, norm_gain, w_gate, w_up, w_down, score_vec):
        width = preview.shape[1]
        dims = (((1,), (1,)), ((), ()))
        owner_lanes = jnp.broadcast_to(row_owner.astype(BF16)[:, None], (row_owner.shape[0], LANES))
        both = gather(jnp.concatenate([preview, owner_lanes], axis=1))
        rows_all = both[:, :width].astype(F32)
        owner = both[:, width].astype(jnp.int32)
        member = (owner[:, None] == jnp.arange(CAND, dtype=jnp.int32)[None, :]).astype(F32)
        x = (rows_all * norm_gain[None, :]).astype(BF16)
        sq = tp_sum(jnp.sum(rows_all * rows_all, axis=1)[:, None])
        scale = lax.rsqrt(sq / (width * tp) + 1e-05)
        units = w_gate.shape[0]
        gate = lax.dot_general(x, w_gate, dims, preferred_element_type=F32).astype(BF16)
        up = lax.dot_general(x, w_up, dims, preferred_element_type=F32).astype(BF16)
        gate_up = tp_sum(jnp.concatenate([gate, up], axis=1)) * scale
        hidden = (jax.nn.silu(gate_up[:, :units]) * gate_up[:, units:]).astype(BF16)
        unit_score = jnp.sum(w_down.astype(F32) * score_vec[None, :], axis=1)
        rows = preview.shape[0]
        row_part = jnp.sum(hidden.astype(F32) * unit_score[None, :], axis=1)
        own_part = jnp.sum(preview.astype(F32) * score_vec[None, :], axis=1)
        totals = jnp.sum(member * row_part[:, None], axis=0) + jnp.sum(member[:rows] * own_part[:, None], axis=0)
        totals = tp_swap(totals) + totals if tp == 2 else lax.psum(totals, "tp")
        totals = sum_sections(totals)
        scores = totals / jnp.sum(member, axis=0)
        down = jnp.dot(hidden, w_down, preferred_element_type=F32).astype(BF16)
        verified = (preview.astype(F32) + scatter(down)).astype(BF16)
        return verified, scores

    return shards


NT = (((1,), (1,)), ((), ()))
VMEM = pl.BlockSpec(memory_space=pltpu.VMEM)
TILE = 256


def call(body, out_shape, args, scratch, megabytes, flops):
    size = sum(a.size * a.dtype.itemsize for a in args)
    return pl.pallas_call(
        body,
        out_shape=out_shape,
        in_specs=[VMEM] * len(args),
        out_specs=jax.tree.map(lambda _: VMEM, out_shape),
        scratch_shapes=scratch,
        compiler_params=pltpu.CompilerParams(vmem_limit_bytes=megabytes << 20),
        cost_estimate=pl.CostEstimate(flops=flops, bytes_accessed=size, transcendentals=0),
    )(*args)


def payload(preview, row_owner, flops):
    rows, width = preview.shape

    def body(rows_ref, owner_ref, out):
        out[:, :width] = rows_ref[...]
        at = lax.broadcasted_iota(jnp.int32, (rows, LANES), 0)
        owner = jnp.zeros((rows, LANES), F32)
        for i in range(rows):
            owner = jnp.where(at == i, owner_ref[i].astype(F32), owner)
        out[:, width:] = owner.astype(BF16)

    return pl.pallas_call(
        body,
        out_shape=pltpu.VMEM((rows, width + LANES), BF16),
        in_specs=[VMEM, pl.BlockSpec(memory_space=pltpu.SMEM)],
        out_specs=VMEM,
        cost_estimate=pl.CostEstimate(flops=flops, bytes_accessed=4 * rows * width, transcendentals=0),
    )(preview, row_owner)


def join(arrays, flops):
    rows = sum(a.shape[0] for a in arrays)

    def body(*refs):
        at = 0
        for ref in refs[:-1]:
            refs[-1][at : at + ref.shape[0], :] = ref[...]
            at += ref.shape[0]

    return call(body, jax.ShapeDtypeStruct((rows, arrays[0].shape[1]), arrays[0].dtype), arrays, [], 4, flops)


def place_rows(pieces, places, gain_ref, x, squares, owner):
    width = x.shape[1]
    for ref, blocks in zip(pieces, places):
        size = ref.shape[0] // len(blocks)
        for i, to in enumerate(blocks):
            v = ref[i * size : (i + 1) * size, :width].astype(F32)
            here = slice(to, to + size)
            owner[here, :] = ref[i * size : (i + 1) * size, width:].astype(F32)
            squares[here, :] = jnp.broadcast_to(jnp.sum(v * v, axis=1, keepdims=True), (size, LANES))
            x[here, :] = (v * gain_ref[...]).astype(BF16)


def early_rows(pieces, places, gain, rows, flops):
    def body(*refs):
        place_rows(refs[: len(pieces)], places, *refs[len(pieces) :])

    lanes = jax.ShapeDtypeStruct((rows, LANES), F32)
    out_shape = (jax.ShapeDtypeStruct((rows, gain.shape[1]), BF16), lanes, lanes)
    return call(body, out_shape, (*pieces, gain), [], 4, flops)


def gate_up(early, early_places, pieces, places, gain, w_gate, w_up):
    rows, width = early[0].shape
    units = w_gate.shape[0]

    def body(x_in, squares_in, owner_in, *refs):
        given = refs[: len(pieces)]
        gain_ref, gate_ref, up_ref, part, squares, owner, x = refs[len(pieces) :]
        for start, stop in early_places:
            for source, to in ((x_in, x), (squares_in, squares), (owner_in, owner)):
                to[start:stop, :] = source[start:stop, :]
        place_rows(given, places, gain_ref, x, squares, owner)

        @pl.loop(0, units // TILE)
        def _(i):
            tile = pl.ds(pl.multiple_of(i * TILE, TILE), TILE)
            for k, w in enumerate((gate_ref, up_ref)):
                part[k, :, tile] = lax.dot_general(x[...], w[tile, :], NT, preferred_element_type=F32).astype(BF16)

    lanes = jax.ShapeDtypeStruct((rows, LANES), F32)
    out_shape = (jax.ShapeDtypeStruct((2, rows, units), BF16), lanes, lanes)
    scratch = [pltpu.VMEM((rows, width), BF16)]
    args = (*early, *pieces, gain, w_gate, w_up)
    return call(body, out_shape, args, scratch, 7, 4 * rows * width * units)


def split_lanes(total, rows):
    high = total.astype(BF16).astype(F32)
    middle = (total - high).astype(BF16).astype(F32)
    low = total - high - middle
    at = lax.broadcasted_iota(jnp.int32, (rows, LANES), 0)
    return jnp.where(at == 0, high, jnp.where(at == 1, middle, jnp.where(at == 2, low, 0.0))).astype(BF16)


def down_rows(mine, theirs, squares, other_squares, owner, w_down, score, own):
    units, width = w_down.shape
    rows = squares.shape[0]
    q = rows // 8
    h = q // 2
    wide = 1024

    def body(a, b, sq, other_sq, owner_ref, w, score_ref, own_ref, *rest):
        near, across, far, (totals, hidden) = rest[:4], rest[4], rest[5:9], rest[9:]
        for block in range(8):
            other = block ^ 3 if block % 4 in (1, 2) else block
            here = slice(block * q, (block + 1) * q)
            there = slice(other * q, (other + 1) * q)
            scale = lax.rsqrt((sq[here, :1] + other_sq[there, :1]) / (2 * width) + 1e-05)
            for lo in range(0, units, TILE):
                cols = slice(lo, lo + TILE)
                g = (a[0, here, cols].astype(F32) + b[0, there, cols].astype(F32)) * scale
                u = (a[1, here, cols].astype(F32) + b[1, there, cols].astype(F32)) * scale
                hidden[here, cols] = (jax.nn.silu(g) * u).astype(BF16)
        row_part = jnp.zeros((rows, 1), F32)
        for lo in range(0, width, wide):
            cols = slice(lo, lo + wide)
            product = jnp.dot(hidden[...], w[:, cols], preferred_element_type=F32)
            product_bf16 = product.astype(BF16)
            for block in range(4):
                at = block * q
                near[block][:, cols] = product_bf16[at : at + h]
                across[block * h : (block + 1) * h, cols] = product_bf16[at + h : at + q]
                far[block][:, cols] = product_bf16[4 * q + at : 5 * q + at]
            row_part += jnp.sum(product * score_ref[:, cols], axis=1, keepdims=True)
        group = owner_ref[...]
        member = group == lax.broadcasted_iota(jnp.int32, group.shape, 1).astype(F32)
        total = jnp.sum(jnp.where(member, row_part, 0.0), axis=0, keepdims=True)
        own_part = jnp.sum(own_ref[:, :width].astype(F32) * score_ref[...], axis=1, keepdims=True)
        total += jnp.sum(jnp.where(member[:h], own_part, 0.0), axis=0, keepdims=True)
        totals[...] = jnp.zeros_like(totals)
        totals[0:1, :] = total
        totals[1:2, :] = jnp.sum(member.astype(F32), axis=0, keepdims=True)
        far[3][:, width:] = split_lanes(total, q)

    shapes = [(h, width)] * 4 + [(4 * h, width)] + [(q, width)] * 3 + [(q, width + LANES)]
    blocks = [jax.ShapeDtypeStruct(shape, BF16) for shape in shapes]
    out_shape = (*blocks, jax.ShapeDtypeStruct((8, LANES), F32))
    args = (mine, theirs, squares, other_squares, owner, w_down, score, own)
    return call(body, out_shape, args, [pltpu.VMEM((rows, units), BF16)], 14, 2 * rows * units * width)


def carried(ref):
    return sum(ref[i : i + 1, ref.shape[1] - LANES :].astype(F32) for i in range(3))


def fold(terms, totals, carriers, cuts, width, flops=0):
    count = len(terms)

    def body(*refs):
        given, totals_ref, brought = refs[:count], refs[count], refs[count + 1 : count + 1 + len(carriers)]
        outs, totals_out = refs[count + 1 + len(carriers) : -1], refs[-1]
        total = totals_ref[0:1, :]
        for ref in brought:
            total += carried(ref)
        totals_out[...] = totals_ref[...]
        totals_out[0:1, :] = total
        for (start, stop, sent), out in zip(cuts, outs):
            for lo in range(start, stop, 16):
                here = slice(lo, lo + 16)
                v = given[0][here, :width].astype(F32)
                for ref in given[1:]:
                    v += ref[here, :width].astype(F32)
                out[lo - start : lo - start + 16, :width] = v.astype(BF16)
            if sent:
                out[:, width:] = split_lanes(total, stop - start)

    shapes = [jax.ShapeDtypeStruct((stop - start, width + (LANES if sent else 0)), BF16) for start, stop, sent in cuts]
    out_shape = (*shapes, jax.ShapeDtypeStruct(totals.shape, F32))
    return call(body, out_shape, (*terms, totals, *carriers), [], 8, flops)


def paired(n, tp):
    def swap(v, even, odd=None):
        odd = even if odd is None else odd
        pairs = [(s * tp + t, (s ^ (odd if t else even)) * tp + t) for s in range(n) for t in range(tp)]
        return lax.ppermute(v, BOTH, pairs)

    def tp_swap(v):
        return lax.ppermute(v, "tp", [(0, 1), (1, 0)])

    after = lax.optimization_barrier

    def shards(preview, row_owner, norm_gain, w_gate, w_up, w_down, score_vec):
        rows = preview.shape[0]
        own = payload(preview, row_owner, 10**10)
        z2 = swap(own, 8)
        own_a, own_b = swap(own, 1, 2), swap(own, 2, 1)
        z3 = swap(z2, 4)
        z2, own_a, own_b = after((join((z2,), 10**10), own_a, own_b))
        z2_a, z2_b = swap(z2, 1, 2), swap(z2, 2, 1)
        own_c = swap(own_a, 2, 1)
        across = swap(join((own, own_a, own_b), 0), 4)
        z3 = join((z3,), 10**10)
        z3_a, z3_b = swap(z3, 1, 2), swap(z3, 2, 1)
        z2_a, own_c = after((join((z2_a,), 10**10), own_c))
        across_c = swap(own_c, 4)
        z2_c = swap(z2_a, 2, 1)
        z3_c = swap(z3_a, 2, 1)

        q, half = 2 * rows, 8 * rows
        gain, score = norm_gain[None, :], score_vec[None, :]
        pieces = [own, own_a, own_b, own_c, across, z2, z2_a, z2_b, z3, z3_a, z3_b]
        places = [(i * q,) for i in range(4)] + [tuple(i * q + rows for i in range(3))]
        places += [(half + i * q,) for i in range(3)] + [(half + i * q + rows,) for i in range(3)]
        early = early_rows(pieces, places, gain, 2 * half, 10**9)
        early_places = [(0, half - rows), (half, half + 3 * q)]
        late_places = [(half - rows,), (half + 3 * q,), (half + 3 * q + rows,)]
        part, squares, owner = gate_up(early, early_places, [across_c, z2_c, z3_c], late_places, gain, w_gate, w_up)
        other, other_squares = tp_swap(part), tp_swap(squares)
        *near, across, f0, f1, f2, f3, totals = down_rows(part, other, squares, other_squares, owner, w_down, score, own)
        width = preview.shape[1]
        counts = totals[1, :CAND]
        f3 = swap(f3, 2, 1)
        across = swap(across, 4)
        f2 = swap(f2, 2, 1)
        send, totals = fold([f1, f3], totals, [f3], [(0, q, True)], width, 2 * 10**9)
        f1 = swap(send, 1, 2)
        f0, _ = fold([f0, f2], totals, [], [(0, q, False)], width, 2 * 10**9)
        keep, send, totals = fold([f0, f1], totals, [f1], [(0, rows, False), (rows, q, True)], width)
        z3 = swap(send, 4)
        near = [add(v, across[i * rows : (i + 1) * rows]) for i, v in enumerate(near)]
        n3, n2 = swap(near[3], 2, 1), swap(near[2], 2, 1)
        send, totals = fold([keep, z3], totals, [z3], [(0, rows, True)], width)
        z2 = swap(send, 8)
        n1 = swap(add(near[1], n3), 1, 2)
        total = totals[0, :] + jnp.sum(z2[:3, width:].astype(F32), axis=0)
        total = total + tp_swap(total)
        verified = own[:, :width].astype(F32) + near[0].astype(F32)
        verified = verified + n2.astype(F32) + n1.astype(F32) + z2[:, :width].astype(F32)
        return verified.astype(BF16), total[:CAND] / counts

    return shards


def solution(mesh):
    n, tp = mesh.shape["section"], mesh.shape["tp"]
    placed = (
        P("section", "tp"),
        P("section"),
        P("tp"),
        P("section", "tp"),
        P("section", "tp"),
        P("section", "tp"),
        P("tp"),
    )
    return jax.shard_map(
        (paired if (n, tp) == (16, 2) else general)(n, tp),
        mesh=mesh,
        in_specs=placed,
        out_specs=(P("section", "tp"), P()),
        check_vma=False,
    )
```

```python
import jax
import jax.numpy as jnp
from jax import lax
from jax.experimental import pallas as pl
from jax.experimental.pallas import tpu as pltpu
from jax.sharding import PartitionSpec as P

CAND = 32
LANES = 128
BOTH = ("section", "tp")
F32 = jnp.float32
BF16 = jnp.bfloat16


def cat(*parts):
    return jnp.concatenate(parts, axis=0)


def add(a, b):
    return (a.astype(F32) + b.astype(F32)).astype(BF16)


def general(n, tp):
    def swap(v, even, odd=None):
        odd = even if odd is None else odd
        pairs = [(s * tp + t, (s ^ (odd if t % 2 else even)) * tp + t) for s in range(n) for t in range(tp)]
        return lax.ppermute(v, BOTH, pairs)

    long_bits = [8 << i for i in range((n // 8).bit_length() - 1)]

    def gather_quad(g):
        a = swap(g, 1, 2)
        g = cat(g, a)
        return cat(g, swap(g, 2, 1))

    def gather(own):
        rows = own.shape[0]
        far = own
        for bit in long_bits:
            far = cat(far, swap(far, bit))
        far = far[rows:]
        near = cat(own, swap(own, 4))
        far = cat(far, swap(far, 4))
        return cat(gather_quad(near), gather_quad(far))

    def swap_middle(v):
        rows = v.shape[0] // n
        out, at = [], 0
        for length in (8 * rows, v.shape[0] - 8 * rows):
            q = length // 4
            out += [v[at + i * q : at + (i + 1) * q] for i in (0, 2, 1, 3)]
            at += length
        return cat(*out)

    def scatter_quad(v):
        h = v.shape[0] // 2
        v = add(v[:h], swap(v[h:], 2, 1))
        h //= 2
        return add(v[:h], swap(v[h:], 1, 2))

    def scatter(v):
        rows = v.shape[0] // n
        far = scatter_quad(v[8 * rows :])
        near = scatter_quad(v[: 8 * rows])
        h = far.shape[0] // 2
        far = add(far[:h], swap(far[h:], 4))
        near = add(near[:rows], swap(near[rows:], 4))
        v = cat(near, far)
        for bit in reversed(long_bits):
            h = v.shape[0] // 2
            got = swap(v[h:], bit)
            v = add(v[:h], got) if h > rows else v[:h].astype(F32) + got.astype(F32)
        return v

    def sum_sections(v):
        for bit in [1 << i for i in range(n.bit_length() - 1)]:
            v = v + swap(v, bit)
        return v

    def tp_swap(v):
        return lax.ppermute(v, "tp", [(t, t ^ 1) for t in range(tp)])

    def tp_sum(v):
        if tp == 2:
            return v.astype(F32) + swap_middle(tp_swap(v)).astype(F32)
        t = lax.axis_index("tp") % 2
        both = lax.psum(jnp.stack([jnp.where(t == 0, v, 0), jnp.where(t == 1, v, 0)]), "tp").astype(F32)
        mine = jnp.where(t == 0, both[0], both[1])
        return mine + swap_middle(jnp.where(t == 0, both[1], both[0]))

    def shards(preview, row_owner, norm_gain, w_gate, w_up, w_down, score_vec):
        width = preview.shape[1]
        dims = (((1,), (1,)), ((), ()))
        owner_lanes = jnp.broadcast_to(row_owner.astype(BF16)[:, None], (row_owner.shape[0], LANES))
        both = gather(jnp.concatenate([preview, owner_lanes], axis=1))
        rows_all = both[:, :width].astype(F32)
        owner = both[:, width].astype(jnp.int32)
        member = (owner[:, None] == jnp.arange(CAND, dtype=jnp.int32)[None, :]).astype(F32)
        x = (rows_all * norm_gain[None, :]).astype(BF16)
        sq = tp_sum(jnp.sum(rows_all * rows_all, axis=1)[:, None])
        scale = lax.rsqrt(sq / (width * tp) + 1e-05)
        units = w_gate.shape[0]
        gate = lax.dot_general(x, w_gate, dims, preferred_element_type=F32).astype(BF16)
        up = lax.dot_general(x, w_up, dims, preferred_element_type=F32).astype(BF16)
        gate_up = tp_sum(jnp.concatenate([gate, up], axis=1)) * scale
        hidden = (jax.nn.silu(gate_up[:, :units]) * gate_up[:, units:]).astype(BF16)
        unit_score = jnp.sum(w_down.astype(F32) * score_vec[None, :], axis=1)
        rows = preview.shape[0]
        row_part = jnp.sum(hidden.astype(F32) * unit_score[None, :], axis=1)
        own_part = jnp.sum(preview.astype(F32) * score_vec[None, :], axis=1)
        totals = jnp.sum(member * row_part[:, None], axis=0) + jnp.sum(member[:rows] * own_part[:, None], axis=0)
        totals = tp_swap(totals) + totals if tp == 2 else lax.psum(totals, "tp")
        totals = sum_sections(totals)
        scores = totals / jnp.sum(member, axis=0)
        down = jnp.dot(hidden, w_down, preferred_element_type=F32).astype(BF16)
        verified = (preview.astype(F32) + scatter(down)).astype(BF16)
        return verified, scores

    return shards


NT = (((1,), (1,)), ((), ()))
VMEM = pl.BlockSpec(memory_space=pltpu.VMEM)
TILE = 256


def call(body, out_shape, args, scratch, megabytes, flops):
    size = sum(a.size * a.dtype.itemsize for a in args)
    return pl.pallas_call(
        body,
        out_shape=out_shape,
        in_specs=[VMEM] * len(args),
        out_specs=jax.tree.map(lambda _: VMEM, out_shape),
        scratch_shapes=scratch,
        compiler_params=pltpu.CompilerParams(vmem_limit_bytes=megabytes << 20),
        cost_estimate=pl.CostEstimate(flops=flops, bytes_accessed=size, transcendentals=0),
    )(*args)


def payload(preview, row_owner, flops):
    rows, width = preview.shape

    def body(rows_ref, owner_ref, out):
        out[:, :width] = rows_ref[...]
        at = lax.broadcasted_iota(jnp.int32, (rows, LANES), 0)
        owner = jnp.zeros((rows, LANES), F32)
        for i in range(rows):
            owner = jnp.where(at == i, owner_ref[i].astype(F32), owner)
        out[:, width:] = owner.astype(BF16)

    return pl.pallas_call(
        body,
        out_shape=pltpu.VMEM((rows, width + LANES), BF16),
        in_specs=[VMEM, pl.BlockSpec(memory_space=pltpu.SMEM)],
        out_specs=VMEM,
        cost_estimate=pl.CostEstimate(flops=flops, bytes_accessed=4 * rows * width, transcendentals=0),
    )(preview, row_owner)


def join(arrays, flops):
    rows = sum(a.shape[0] for a in arrays)

    def body(*refs):
        at = 0
        for ref in refs[:-1]:
            refs[-1][at : at + ref.shape[0], :] = ref[...]
            at += ref.shape[0]

    return call(body, jax.ShapeDtypeStruct((rows, arrays[0].shape[1]), arrays[0].dtype), arrays, [], 4, flops)


def place_rows(pieces, places, gain_ref, x, squares, owner):
    width = x.shape[1]
    for ref, blocks in zip(pieces, places):
        size = ref.shape[0] // len(blocks)
        for i, to in enumerate(blocks):
            v = ref[i * size : (i + 1) * size, :width].astype(F32)
            here = slice(to, to + size)
            owner[here, :] = ref[i * size : (i + 1) * size, width:].astype(F32)
            squares[here, :] = jnp.broadcast_to(jnp.sum(v * v, axis=1, keepdims=True), (size, LANES))
            x[here, :] = (v * gain_ref[...]).astype(BF16)


def early_rows(pieces, places, gain, rows, flops):
    def body(*refs):
        place_rows(refs[: len(pieces)], places, *refs[len(pieces) :])

    lanes = jax.ShapeDtypeStruct((rows, LANES), F32)
    out_shape = (jax.ShapeDtypeStruct((rows, gain.shape[1]), BF16), lanes, lanes)
    return call(body, out_shape, (*pieces, gain), [], 4, flops)


def gate_up(early, early_places, pieces, places, gain, w_gate, w_up):
    rows, width = early[0].shape
    units = w_gate.shape[0]
    first_units = 5 * TILE

    def body(x_in, squares_in, owner_in, *refs):
        given = refs[: len(pieces)]
        gain_ref, gate_ref, up_ref, head, tail, owner, x, squares = refs[len(pieces) :]
        for start, stop in early_places:
            for source, to in ((x_in, x), (squares_in, squares), (owner_in, owner)):
                to[start:stop, :] = source[start:stop, :]
        place_rows(given, places, gain_ref, x, squares, owner)

        total = squares[...]
        high = total.astype(BF16).astype(F32)
        middle = (total - high).astype(BF16).astype(F32)
        low = total - high - middle
        at = lax.broadcasted_iota(jnp.int32, (rows, LANES), 1)
        pieces_of = jnp.where(at == 0, high, jnp.where(at == 1, middle, jnp.where(at == 2, low, 0.0)))
        head[0, :, first_units:] = pieces_of.astype(BF16)
        head[1, :, first_units:] = jnp.zeros((rows, LANES), BF16)
        for part, first in ((head, 0), (tail, first_units)):

            @pl.loop(0, part.shape[2] // TILE)
            def _(i):
                tile = pl.ds(pl.multiple_of(i * TILE, TILE), TILE)
                row = pl.ds(pl.multiple_of(first + i * TILE, TILE), TILE)
                for k, w in enumerate((gate_ref, up_ref)):
                    part[k, :, tile] = lax.dot_general(x[...], w[row, :], NT, preferred_element_type=F32).astype(BF16)

    lanes = jax.ShapeDtypeStruct((rows, LANES), F32)
    parts = [jax.ShapeDtypeStruct((2, rows, n), BF16) for n in (first_units + LANES, units - first_units)]
    out_shape = (*parts, lanes)
    scratch = [pltpu.VMEM((rows, width), BF16), pltpu.VMEM((rows, LANES), F32)]
    args = (*early, *pieces, gain, w_gate, w_up)
    return call(body, out_shape, args, scratch, 7, 4 * rows * width * units)


def hidden_units(part, other, scales, hidden):
    units = hidden.shape[1]
    q = hidden.shape[0] // 8
    for block in range(8):
        mate = block ^ 3 if block % 4 in (1, 2) else block
        here = slice(block * q, (block + 1) * q)
        there = slice(mate * q, (mate + 1) * q)
        scale = scales[here, :1]
        for lo in range(0, units, TILE):
            cols = slice(lo, lo + TILE)
            g = (part[0, here, cols].astype(F32) + other[0, there, cols].astype(F32)) * scale
            u = (part[1, here, cols].astype(F32) + other[1, there, cols].astype(F32)) * scale
            hidden[here, cols] = (jax.nn.silu(g) * u).astype(BF16)


def first_hidden(part, other, width):
    rows, units = part.shape[1], part.shape[2] - LANES
    q = rows // 8

    def body(part_ref, other_ref, hidden, scales):
        for block in range(8):
            mate = block ^ 3 if block % 4 in (1, 2) else block
            here = slice(block * q, (block + 1) * q)
            there = slice(mate * q, (mate + 1) * q)
            squares = part_ref[0, here, units:].astype(F32) + other_ref[0, there, units:].astype(F32)
            scale = lax.rsqrt(jnp.sum(squares, axis=1, keepdims=True) / (2 * width) + 1e-05)
            scales[here, :] = jnp.broadcast_to(scale, (q, LANES))
        hidden_units(part_ref, other_ref, scales, hidden)

    out_shape = (jax.ShapeDtypeStruct((rows, units), BF16), jax.ShapeDtypeStruct((rows, LANES), F32))
    return call(body, out_shape, (part, other), [], 4, 10**8)


def split_lanes(total, rows):
    high = total.astype(BF16).astype(F32)
    middle = (total - high).astype(BF16).astype(F32)
    low = total - high - middle
    at = lax.broadcasted_iota(jnp.int32, (rows, LANES), 0)
    return jnp.where(at == 0, high, jnp.where(at == 1, middle, jnp.where(at == 2, low, 0.0))).astype(BF16)


def down_rows(first, mine, theirs, scales, owner, w_down, score, own):
    units, width = w_down.shape
    rows = owner.shape[0]
    q = rows // 8
    h = q // 2
    wide = 1024
    split = first.shape[1]

    def body(first_ref, a, b, scales_ref, owner_ref, w, score_ref, own_ref, *rest):
        near, across, far, (totals, hidden) = rest[:4], rest[4], rest[5:9], rest[9:]
        hidden_units(a, b, scales_ref, hidden)
        row_part = jnp.zeros((rows, 1), F32)
        for lo in range(0, width, wide):
            cols = slice(lo, lo + wide)
            product = jnp.dot(first_ref[...], w[:split, cols], preferred_element_type=F32)
            product += jnp.dot(hidden[...], w[split:, cols], preferred_element_type=F32)
            product_bf16 = product.astype(BF16)
            for block in range(4):
                at = block * q
                near[block][:, cols] = product_bf16[at : at + h]
                across[block * h : (block + 1) * h, cols] = product_bf16[at + h : at + q]
                far[block][:, cols] = product_bf16[4 * q + at : 5 * q + at]
            row_part += jnp.sum(product * score_ref[:, cols], axis=1, keepdims=True)
        group = owner_ref[...]
        member = group == lax.broadcasted_iota(jnp.int32, group.shape, 1).astype(F32)
        total = jnp.sum(jnp.where(member, row_part, 0.0), axis=0, keepdims=True)
        own_part = jnp.sum(own_ref[:, :width].astype(F32) * score_ref[...], axis=1, keepdims=True)
        total += jnp.sum(jnp.where(member[:h], own_part, 0.0), axis=0, keepdims=True)
        totals[...] = jnp.zeros_like(totals)
        totals[0:1, :] = total
        totals[1:2, :] = jnp.sum(member.astype(F32), axis=0, keepdims=True)
        far[3][:, width:] = split_lanes(total, q)

    shapes = [(h, width)] * 4 + [(4 * h, width)] + [(q, width)] * 3 + [(q, width + LANES)]
    blocks = [jax.ShapeDtypeStruct(shape, BF16) for shape in shapes]
    out_shape = (*blocks, jax.ShapeDtypeStruct((8, LANES), F32))
    args = (first, mine, theirs, scales, owner, w_down, score, own)
    return call(body, out_shape, args, [pltpu.VMEM((rows, units - split), BF16)], 14, 2 * rows * units * width)


def carried(ref):
    return sum(ref[i : i + 1, ref.shape[1] - LANES :].astype(F32) for i in range(3))


def fold(terms, totals, carriers, cuts, width, flops=0):
    count = len(terms)

    def body(*refs):
        given, totals_ref, brought = refs[:count], refs[count], refs[count + 1 : count + 1 + len(carriers)]
        outs, totals_out = refs[count + 1 + len(carriers) : -1], refs[-1]
        total = totals_ref[0:1, :]
        for ref in brought:
            total += carried(ref)
        totals_out[...] = totals_ref[...]
        totals_out[0:1, :] = total
        for (start, stop, sent), out in zip(cuts, outs):
            for lo in range(start, stop, 16):
                here = slice(lo, lo + 16)
                v = given[0][here, :width].astype(F32)
                for ref in given[1:]:
                    v += ref[here, :width].astype(F32)
                out[lo - start : lo - start + 16, :width] = v.astype(BF16)
            if sent:
                out[:, width:] = split_lanes(total, stop - start)

    shapes = [jax.ShapeDtypeStruct((stop - start, width + (LANES if sent else 0)), BF16) for start, stop, sent in cuts]
    out_shape = (*shapes, jax.ShapeDtypeStruct(totals.shape, F32))
    return call(body, out_shape, (*terms, totals, *carriers), [], 8, flops)


def paired(n, tp):
    def swap(v, even, odd=None):
        odd = even if odd is None else odd
        pairs = [(s * tp + t, (s ^ (odd if t else even)) * tp + t) for s in range(n) for t in range(tp)]
        return lax.ppermute(v, BOTH, pairs)

    def tp_swap(v):
        return lax.ppermute(v, "tp", [(0, 1), (1, 0)])

    after = lax.optimization_barrier

    def shards(preview, row_owner, norm_gain, w_gate, w_up, w_down, score_vec):
        rows = preview.shape[0]
        own = payload(preview, row_owner, 10**10)
        z2 = swap(own, 8)
        own_a, own_b = swap(own, 1, 2), swap(own, 2, 1)
        z3 = swap(z2, 4)
        z2, own_a, own_b = after((join((z2,), 10**10), own_a, own_b))
        z2_a, z2_b = swap(z2, 1, 2), swap(z2, 2, 1)
        own_c = swap(own_a, 2, 1)
        across = swap(join((own, own_a, own_b), 0), 4)
        z3 = join((z3,), 10**10)
        z3_a, z3_b = swap(z3, 1, 2), swap(z3, 2, 1)
        z2_a, own_c = after((join((z2_a,), 10**10), own_c))
        across_c = swap(own_c, 4)
        z2_c = swap(z2_a, 2, 1)
        z3_c = swap(z3_a, 2, 1)

        q, half = 2 * rows, 8 * rows
        gain, score = norm_gain[None, :], score_vec[None, :]
        pieces = [own, own_a, own_b, own_c, across, z2, z2_a, z2_b, z3, z3_a, z3_b]
        places = [(i * q,) for i in range(4)] + [tuple(i * q + rows for i in range(3))]
        places += [(half + i * q,) for i in range(3)] + [(half + i * q + rows,) for i in range(3)]
        early = early_rows(pieces, places, gain, 2 * half, 10**9)
        early_places = [(0, half - rows), (half, half + 3 * q)]
        late_places = [(half - rows,), (half + 3 * q,), (half + 3 * q + rows,)]
        late = [across_c, z2_c, z3_c]
        head, tail, owner = gate_up(early, early_places, late, late_places, gain, w_gate, w_up)
        other_head, other_tail = tp_swap(head), tp_swap(tail)
        first, scales = first_hidden(head, other_head, preview.shape[1])
        *near, across, f0, f1, f2, f3, totals = down_rows(
            first, tail, other_tail, scales, owner, w_down, score, own
        )
        width = preview.shape[1]
        counts = totals[1, :CAND]
        f3 = swap(f3, 2, 1)
        across = swap(across, 4)
        f2 = swap(f2, 2, 1)
        send, totals = fold([f1, f3], totals, [f3], [(0, q, True)], width, 2 * 10**9)
        f1 = swap(send, 1, 2)
        f0, _ = fold([f0, f2], totals, [], [(0, q, False)], width, 2 * 10**9)
        keep, send, totals = fold([f0, f1], totals, [f1], [(0, rows, False), (rows, q, True)], width)
        z3 = swap(send, 4)
        near = [add(v, across[i * rows : (i + 1) * rows]) for i, v in enumerate(near)]
        n3, n2 = swap(near[3], 2, 1), swap(near[2], 2, 1)
        send, totals = fold([keep, z3], totals, [z3], [(0, rows, True)], width)
        z2 = swap(send, 8)
        n1 = swap(add(near[1], n3), 1, 2)
        total = totals[0, :] + jnp.sum(z2[:3, width:].astype(F32), axis=0)
        total = total + tp_swap(total)
        verified = own[:, :width].astype(F32) + near[0].astype(F32)
        verified = verified + n2.astype(F32) + n1.astype(F32) + z2[:, :width].astype(F32)
        return verified.astype(BF16), total[:CAND] / counts

    return shards


def solution(mesh):
    n, tp = mesh.shape["section"], mesh.shape["tp"]
    placed = (
        P("section", "tp"),
        P("section"),
        P("tp"),
        P("section", "tp"),
        P("section", "tp"),
        P("section", "tp"),
        P("tp"),
    )
    return jax.shard_map(
        (paired if (n, tp) == (16, 2) else general)(n, tp),
        mesh=mesh,
        in_specs=placed,
        out_specs=(P("section", "tp"), P()),
        check_vma=False,
    )
```

```python
import jax
import jax.numpy as jnp
from jax import lax
from jax.experimental import pallas as pl
from jax.experimental.pallas import tpu as pltpu
from jax.sharding import PartitionSpec as P

CAND = 32
LANES = 128
BOTH = ("section", "tp")
F32 = jnp.float32
BF16 = jnp.bfloat16


def cat(*parts):
    return jnp.concatenate(parts, axis=0)


def add(a, b):
    return (a.astype(F32) + b.astype(F32)).astype(BF16)


def general(n, tp):
    def swap(v, even, odd=None):
        odd = even if odd is None else odd
        pairs = [(s * tp + t, (s ^ (odd if t % 2 else even)) * tp + t) for s in range(n) for t in range(tp)]
        return lax.ppermute(v, BOTH, pairs)

    long_bits = [8 << i for i in range((n // 8).bit_length() - 1)]

    def gather_quad(g):
        a = swap(g, 1, 2)
        g = cat(g, a)
        return cat(g, swap(g, 2, 1))

    def gather(own):
        rows = own.shape[0]
        far = own
        for bit in long_bits:
            far = cat(far, swap(far, bit))
        far = far[rows:]
        near = cat(own, swap(own, 4))
        far = cat(far, swap(far, 4))
        return cat(gather_quad(near), gather_quad(far))

    def swap_middle(v):
        rows = v.shape[0] // n
        out, at = [], 0
        for length in (8 * rows, v.shape[0] - 8 * rows):
            q = length // 4
            out += [v[at + i * q : at + (i + 1) * q] for i in (0, 2, 1, 3)]
            at += length
        return cat(*out)

    def scatter_quad(v):
        h = v.shape[0] // 2
        v = add(v[:h], swap(v[h:], 2, 1))
        h //= 2
        return add(v[:h], swap(v[h:], 1, 2))

    def scatter(v):
        rows = v.shape[0] // n
        far = scatter_quad(v[8 * rows :])
        near = scatter_quad(v[: 8 * rows])
        h = far.shape[0] // 2
        far = add(far[:h], swap(far[h:], 4))
        near = add(near[:rows], swap(near[rows:], 4))
        v = cat(near, far)
        for bit in reversed(long_bits):
            h = v.shape[0] // 2
            got = swap(v[h:], bit)
            v = add(v[:h], got) if h > rows else v[:h].astype(F32) + got.astype(F32)
        return v

    def sum_sections(v):
        for bit in [1 << i for i in range(n.bit_length() - 1)]:
            v = v + swap(v, bit)
        return v

    def tp_swap(v):
        return lax.ppermute(v, "tp", [(t, t ^ 1) for t in range(tp)])

    def tp_sum(v):
        if tp == 2:
            return v.astype(F32) + swap_middle(tp_swap(v)).astype(F32)
        t = lax.axis_index("tp") % 2
        both = lax.psum(jnp.stack([jnp.where(t == 0, v, 0), jnp.where(t == 1, v, 0)]), "tp").astype(F32)
        mine = jnp.where(t == 0, both[0], both[1])
        return mine + swap_middle(jnp.where(t == 0, both[1], both[0]))

    def shards(preview, row_owner, norm_gain, w_gate, w_up, w_down, score_vec):
        width = preview.shape[1]
        dims = (((1,), (1,)), ((), ()))
        owner_lanes = jnp.broadcast_to(row_owner.astype(BF16)[:, None], (row_owner.shape[0], LANES))
        both = gather(jnp.concatenate([preview, owner_lanes], axis=1))
        rows_all = both[:, :width].astype(F32)
        owner = both[:, width].astype(jnp.int32)
        member = (owner[:, None] == jnp.arange(CAND, dtype=jnp.int32)[None, :]).astype(F32)
        x = (rows_all * norm_gain[None, :]).astype(BF16)
        sq = tp_sum(jnp.sum(rows_all * rows_all, axis=1)[:, None])
        scale = lax.rsqrt(sq / (width * tp) + 1e-05)
        units = w_gate.shape[0]
        gate = lax.dot_general(x, w_gate, dims, preferred_element_type=F32).astype(BF16)
        up = lax.dot_general(x, w_up, dims, preferred_element_type=F32).astype(BF16)
        gate_up = tp_sum(jnp.concatenate([gate, up], axis=1)) * scale
        hidden = (jax.nn.silu(gate_up[:, :units]) * gate_up[:, units:]).astype(BF16)
        unit_score = jnp.sum(w_down.astype(F32) * score_vec[None, :], axis=1)
        rows = preview.shape[0]
        row_part = jnp.sum(hidden.astype(F32) * unit_score[None, :], axis=1)
        own_part = jnp.sum(preview.astype(F32) * score_vec[None, :], axis=1)
        totals = jnp.sum(member * row_part[:, None], axis=0) + jnp.sum(member[:rows] * own_part[:, None], axis=0)
        totals = tp_swap(totals) + totals if tp == 2 else lax.psum(totals, "tp")
        totals = sum_sections(totals)
        scores = totals / jnp.sum(member, axis=0)
        down = jnp.dot(hidden, w_down, preferred_element_type=F32).astype(BF16)
        verified = (preview.astype(F32) + scatter(down)).astype(BF16)
        return verified, scores

    return shards


NT = (((1,), (1,)), ((), ()))
VMEM = pl.BlockSpec(memory_space=pltpu.VMEM)
TILE = 256


def call(body, out_shape, args, scratch, megabytes, flops):
    size = sum(a.size * a.dtype.itemsize for a in args)
    return pl.pallas_call(
        body,
        out_shape=out_shape,
        in_specs=[VMEM] * len(args),
        out_specs=jax.tree.map(lambda _: VMEM, out_shape),
        scratch_shapes=scratch,
        compiler_params=pltpu.CompilerParams(vmem_limit_bytes=megabytes << 20),
        cost_estimate=pl.CostEstimate(flops=flops, bytes_accessed=size, transcendentals=0),
    )(*args)


def payload(preview, row_owner, flops):
    rows, width = preview.shape

    def body(rows_ref, owner_ref, out):
        out[:, :width] = rows_ref[...]
        at = lax.broadcasted_iota(jnp.int32, (rows, LANES), 0)
        owner = jnp.zeros((rows, LANES), F32)
        for i in range(rows):
            owner = jnp.where(at == i, owner_ref[i].astype(F32), owner)
        out[:, width:] = owner.astype(BF16)

    return pl.pallas_call(
        body,
        out_shape=pltpu.VMEM((rows, width + LANES), BF16),
        in_specs=[VMEM, pl.BlockSpec(memory_space=pltpu.SMEM)],
        out_specs=VMEM,
        cost_estimate=pl.CostEstimate(flops=flops, bytes_accessed=4 * rows * width, transcendentals=0),
    )(preview, row_owner)


def join(arrays, flops):
    rows = sum(a.shape[0] for a in arrays)

    def body(*refs):
        at = 0
        for ref in refs[:-1]:
            refs[-1][at : at + ref.shape[0], :] = ref[...]
            at += ref.shape[0]

    return call(body, jax.ShapeDtypeStruct((rows, arrays[0].shape[1]), arrays[0].dtype), arrays, [], 4, flops)


def place_rows(pieces, places, gain_ref, x, squares, owner):
    width = x.shape[1]
    for ref, blocks in zip(pieces, places):
        size = ref.shape[0] // len(blocks)
        for i, to in enumerate(blocks):
            v = ref[i * size : (i + 1) * size, :width].astype(F32)
            here = slice(to, to + size)
            owner[here, :] = ref[i * size : (i + 1) * size, width:].astype(F32)
            squares[here, :] = jnp.broadcast_to(jnp.sum(v * v, axis=1, keepdims=True), (size, LANES))
            x[here, :] = (v * gain_ref[...]).astype(BF16)


def early_rows(pieces, places, gain, rows, flops):
    def body(*refs):
        place_rows(refs[: len(pieces)], places, *refs[len(pieces) :])

    lanes = jax.ShapeDtypeStruct((rows, LANES), F32)
    out_shape = (jax.ShapeDtypeStruct((rows, gain.shape[1]), BF16), lanes, lanes)
    return call(body, out_shape, (*pieces, gain), [], 4, flops)


def gate_up(early, early_places, pieces, places, gain, w_gate, w_up):
    rows, width = early[0].shape
    units = w_gate.shape[0]
    first_units = 5 * TILE

    def body(x_in, squares_in, owner_in, *refs):
        given = refs[: len(pieces)]
        gain_ref, gate_ref, up_ref, head, tail, owner, x, squares = refs[len(pieces) :]
        for start, stop in early_places:
            for source, to in ((x_in, x), (squares_in, squares), (owner_in, owner)):
                to[start:stop, :] = source[start:stop, :]
        place_rows(given, places, gain_ref, x, squares, owner)

        total = squares[...]
        high = total.astype(BF16).astype(F32)
        middle = (total - high).astype(BF16).astype(F32)
        low = total - high - middle
        at = lax.broadcasted_iota(jnp.int32, (rows, LANES), 1)
        pieces_of = jnp.where(at == 0, high, jnp.where(at == 1, middle, jnp.where(at == 2, low, 0.0)))
        head[0, :, first_units:] = pieces_of.astype(BF16)
        head[1, :, first_units:] = jnp.zeros((rows, LANES), BF16)
        for part, first in ((head, 0), (tail, first_units)):

            @pl.loop(0, part.shape[2] // TILE)
            def _(i):
                tile = pl.ds(pl.multiple_of(i * TILE, TILE), TILE)
                row = pl.ds(pl.multiple_of(first + i * TILE, TILE), TILE)
                for k, w in enumerate((gate_ref, up_ref)):
                    part[k, :, tile] = lax.dot_general(x[...], w[row, :], NT, preferred_element_type=F32).astype(BF16)

    lanes = jax.ShapeDtypeStruct((rows, LANES), F32)
    parts = [jax.ShapeDtypeStruct((2, rows, n), BF16) for n in (first_units + LANES, units - first_units)]
    out_shape = (*parts, lanes)
    scratch = [pltpu.VMEM((rows, width), BF16), pltpu.VMEM((rows, LANES), F32)]
    args = (*early, *pieces, gain, w_gate, w_up)
    return call(body, out_shape, args, scratch, 7, 4 * rows * width * units)


def hidden_units(part, other, scales, hidden):
    units = hidden.shape[1]
    q = hidden.shape[0] // 8
    for block in range(8):
        mate = block ^ 3 if block % 4 in (1, 2) else block
        here = slice(block * q, (block + 1) * q)
        there = slice(mate * q, (mate + 1) * q)
        scale = scales[here, :1]
        for lo in range(0, units, TILE):
            cols = slice(lo, lo + TILE)
            g = (part[0, here, cols].astype(F32) + other[0, there, cols].astype(F32)) * scale
            u = (part[1, here, cols].astype(F32) + other[1, there, cols].astype(F32)) * scale
            hidden[here, cols] = (jax.nn.silu(g) * u).astype(BF16)


def first_hidden(part, other, width):
    rows, units = part.shape[1], part.shape[2] - LANES
    q = rows // 8

    def body(part_ref, other_ref, hidden, scales):
        for block in range(8):
            mate = block ^ 3 if block % 4 in (1, 2) else block
            here = slice(block * q, (block + 1) * q)
            there = slice(mate * q, (mate + 1) * q)
            squares = part_ref[0, here, units:].astype(F32) + other_ref[0, there, units:].astype(F32)
            scale = lax.rsqrt(jnp.sum(squares, axis=1, keepdims=True) / (2 * width) + 1e-05)
            scales[here, :] = jnp.broadcast_to(scale, (q, LANES))
        hidden_units(part_ref, other_ref, scales, hidden)

    out_shape = (jax.ShapeDtypeStruct((rows, units), BF16), jax.ShapeDtypeStruct((rows, LANES), F32))
    return call(body, out_shape, (part, other), [], 4, 10**8)


def split_lanes(total, rows):
    high = total.astype(BF16).astype(F32)
    middle = (total - high).astype(BF16).astype(F32)
    low = total - high - middle
    at = lax.broadcasted_iota(jnp.int32, (rows, LANES), 0)
    return jnp.where(at == 0, high, jnp.where(at == 1, middle, jnp.where(at == 2, low, 0.0))).astype(BF16)


def down_rows(first, mine, theirs, scales, owner, w_down, score, own):
    units, width = w_down.shape
    rows = owner.shape[0]
    q = rows // 8
    h = q // 2
    wide = 1024
    split = first.shape[1]

    def body(first_ref, a, b, scales_ref, owner_ref, w, score_ref, own_ref, *rest):
        near, across, far, (totals, hidden) = rest[:4], rest[4], rest[5:9], rest[9:]
        hidden_units(a, b, scales_ref, hidden)
        row_part = jnp.zeros((rows, 1), F32)
        for lo in range(0, width, wide):
            cols = slice(lo, lo + wide)
            product = jnp.dot(first_ref[...], w[:split, cols], preferred_element_type=F32)
            product += jnp.dot(hidden[...], w[split:, cols], preferred_element_type=F32)
            product_bf16 = product.astype(BF16)
            for block in range(4):
                at = block * q
                near[block][:, cols] = product_bf16[at : at + h]
                across[block * h : (block + 1) * h, cols] = product_bf16[at + h : at + q]
                far[block][:, cols] = product_bf16[4 * q + at : 5 * q + at]
            row_part += jnp.sum(product * score_ref[:, cols], axis=1, keepdims=True)
        group = owner_ref[...]
        member = group == lax.broadcasted_iota(jnp.int32, group.shape, 1).astype(F32)
        total = jnp.sum(jnp.where(member, row_part, 0.0), axis=0, keepdims=True)
        own_part = jnp.sum(own_ref[:, :width].astype(F32) * score_ref[...], axis=1, keepdims=True)
        total += jnp.sum(jnp.where(member[:h], own_part, 0.0), axis=0, keepdims=True)
        totals[...] = jnp.zeros_like(totals)
        totals[0:1, :] = total
        totals[1:2, :] = jnp.sum(member.astype(F32), axis=0, keepdims=True)
        far[3][:, width:] = split_lanes(total, q)

    shapes = [(h, width)] * 4 + [(4 * h, width)] + [(q, width)] * 3 + [(q, width + LANES)]
    blocks = [jax.ShapeDtypeStruct(shape, BF16) for shape in shapes]
    out_shape = (*blocks, jax.ShapeDtypeStruct((8, LANES), F32))
    args = (first, mine, theirs, scales, owner, w_down, score, own)
    return call(body, out_shape, args, [pltpu.VMEM((rows, units - split), BF16)], 14, 2 * rows * units * width)


def carried(ref):
    return sum(ref[i : i + 1, ref.shape[1] - LANES :].astype(F32) for i in range(3))


def fold(terms, totals, carriers, cuts, width, flops=0):
    count = len(terms)

    def body(*refs):
        given, totals_ref, brought = refs[:count], refs[count], refs[count + 1 : count + 1 + len(carriers)]
        outs, totals_out = refs[count + 1 + len(carriers) : -1], refs[-1]
        total = totals_ref[0:1, :]
        for ref in brought:
            total += carried(ref)
        totals_out[...] = totals_ref[...]
        totals_out[0:1, :] = total
        for (start, stop, sent), out in zip(cuts, outs):
            for lo in range(start, stop, 16):
                here = slice(lo, lo + 16)
                v = given[0][here, :width].astype(F32)
                for ref in given[1:]:
                    v += ref[here, :width].astype(F32)
                out[lo - start : lo - start + 16, :width] = v.astype(BF16)
            if sent:
                out[:, width:] = split_lanes(total, stop - start)

    shapes = [jax.ShapeDtypeStruct((stop - start, width + (LANES if sent else 0)), BF16) for start, stop, sent in cuts]
    out_shape = (*shapes, jax.ShapeDtypeStruct(totals.shape, F32))
    return call(body, out_shape, (*terms, totals, *carriers), [], 8, flops)


def paired(n, tp):
    def swap(v, even, odd=None):
        odd = even if odd is None else odd
        pairs = [(s * tp + t, (s ^ (odd if t else even)) * tp + t) for s in range(n) for t in range(tp)]
        return lax.ppermute(v, BOTH, pairs)

    def tp_swap(v):
        return lax.ppermute(v, "tp", [(0, 1), (1, 0)])

    after = lax.optimization_barrier

    def shards(preview, row_owner, norm_gain, w_gate, w_up, w_down, score_vec):
        rows = preview.shape[0]
        own = payload(preview, row_owner, 10**10)
        z2 = swap(own, 8)
        own_a, own_b = swap(own, 1, 2), swap(own, 2, 1)
        z3 = swap(z2, 4)
        z2, own_a, own_b = after((join((z2,), 10**10), own_a, own_b))
        z2_a, z2_b = swap(z2, 1, 2), swap(z2, 2, 1)
        own_c = swap(own_a, 2, 1)
        across = swap(join((own, own_a, own_b), 0), 4)
        z3 = join((z3,), 10**10)
        z3_a, z3_b = swap(z3, 1, 2), swap(z3, 2, 1)
        z2_a, own_c = after((join((z2_a,), 10**10), own_c))
        across_c = swap(own_c, 4)
        z2_c = swap(z2_a, 2, 1)
        z3_c = swap(z3_a, 2, 1)

        q, half = 2 * rows, 8 * rows
        gain, score = norm_gain[None, :], score_vec[None, :]
        pieces = [own, own_a, own_b, own_c, across, z2, z2_a, z2_b, z3, z3_a, z3_b]
        places = [(i * q,) for i in range(4)] + [tuple(i * q + rows for i in range(3))]
        places += [(half + i * q,) for i in range(3)] + [(half + i * q + rows,) for i in range(3)]
        early = early_rows(pieces, places, gain, 2 * half, 2 * 10**8)
        early_places = [(0, half - rows), (half, half + 3 * q)]
        late_places = [(half - rows,), (half + 3 * q,), (half + 3 * q + rows,)]
        late = [across_c, z2_c, z3_c]
        head, tail, owner = gate_up(early, early_places, late, late_places, gain, w_gate, w_up)
        other_head, other_tail = tp_swap(head), tp_swap(tail)
        first, scales = first_hidden(head, other_head, preview.shape[1])
        *near, across, f0, f1, f2, f3, totals = down_rows(
            first, tail, other_tail, scales, owner, w_down, score, own
        )
        width = preview.shape[1]
        counts = totals[1, :CAND]
        f3 = swap(f3, 2, 1)
        across = swap(across, 4)
        f2 = swap(f2, 2, 1)
        send, totals = fold([f1, f3], totals, [f3], [(0, q, True)], width, 2 * 10**9)
        f1 = swap(send, 1, 2)
        f0, _ = fold([f0, f2], totals, [], [(0, q, False)], width, 2 * 10**9)
        keep, send, totals = fold([f0, f1], totals, [f1], [(0, rows, False), (rows, q, True)], width)
        z3 = swap(send, 4)
        near = [add(v, across[i * rows : (i + 1) * rows]) for i, v in enumerate(near)]
        n3, n2 = swap(near[3], 2, 1), swap(near[2], 2, 1)
        send, totals = fold([keep, z3], totals, [z3], [(0, rows, True)], width)
        z2 = swap(send, 8)
        n1 = swap(add(near[1], n3), 1, 2)
        total = totals[0, :] + jnp.sum(z2[:3, width:].astype(F32), axis=0)
        total = total + tp_swap(total)
        verified = own[:, :width].astype(F32) + near[0].astype(F32)
        verified = verified + n2.astype(F32) + n1.astype(F32) + z2[:, :width].astype(F32)
        return verified.astype(BF16), total[:CAND] / counts

    return shards


def solution(mesh):
    n, tp = mesh.shape["section"], mesh.shape["tp"]
    placed = (
        P("section", "tp"),
        P("section"),
        P("tp"),
        P("section", "tp"),
        P("section", "tp"),
        P("section", "tp"),
        P("tp"),
    )
    return jax.shard_map(
        (paired if (n, tp) == (16, 2) else general)(n, tp),
        mesh=mesh,
        in_specs=placed,
        out_specs=(P("section", "tp"), P()),
        check_vma=False,
    )
```
